256 devices in a mesh: clusters: 4 (over x_lo, core), members: 64 (over x_hi, z, y).
Axes of the slice: x: 4 (x_hi: 2, x_lo: 2; x = x_hi * 2 + x_lo), y: 4, z: 8, core: 2. Of those that a mesh axis runs over, the one named last changes fastest.
Arguments:
- embeddings: bfloat16 [65536, 768], P(('clusters', 'members')), parts along dimension 0, may hold values from -400 to 400
- ranks: int32 [65536], P(('clusters', 'members')), parts along dimension 0, may hold values from 0 to 16383, as said below
Outputs:
- max_similarity: float32 [65536], P(('clusters', 'members')), parts along dimension 0
The draws below stay inside these ranges and needn't reach their ends.
There are 4 independent parts, one for each index of `clusters`. The reference program is written for one: setup_inputs(seed, part) draws one part's arguments, and reference() takes and returns one part's arrays. A program takes and returns all parts, laid end to end along the dimension named above; each array names one. Nothing has to cross between parts.
Inputs may be any that keep to these rules, and one draw needn't show every extreme that they name: The rows 256 * b to 256 * (b + 1) - 1 hold the ranks 256 * b to 256 * (b + 1) - 1, each once, in some order.
All inputs are finite; a program needn't handle non-finite values.
Results may differ from the reference program's by a relative error of at most 0.00053.
Values may be sent and summed in bfloat16 or wider, within the bound.
No kernel may reach another device: no remote copies, remote signals or barrier semaphores. Data moves between devices by JAX's collectives and lax.ppermute only.
A program may use at most 64 MiB of HBM per device.

```python
import math
import jax
import jax.numpy as jnp
from jax import lax

D = 768
ROWS_DEV = 256
ROWS = 16384


def draw_embeddings(key, part):
    key = jax.random.fold_in(key, 11)
    keys = jax.random.split(key, 4)
    base = jnp.clip(jax.random.normal(keys[0], (ROWS, D), jnp.float32), -6.0, 6.0)
    source = jax.random.randint(keys[1], (ROWS,), 0, ROWS)
    weight = jnp.exp(jax.random.uniform(keys[2], (ROWS, 1), jnp.float32, math.log(0.5), math.log(4.0)))
    scale = jnp.exp(jax.random.uniform(keys[3], (ROWS, 1), jnp.float32, 0.0, math.log(10.0)))
    return ((base + weight * base[source]) * scale).astype(jnp.bfloat16)


def draw_ranks(key, part):
    key = jax.random.fold_in(key, 23)
    count = ROWS // ROWS_DEV
    keys = jax.random.split(key, count)
    orders = jax.vmap(lambda single: jax.random.permutation(single, ROWS_DEV))(keys)
    offsets = jnp.arange(count, dtype=jnp.int32)[:, None] * ROWS_DEV
    return (orders.astype(jnp.int32) + offsets).reshape(ROWS).astype(jnp.int32)


def setup_inputs(seed: int = 0, part: int = 0) -> dict:
    key_list = jax.random.split(jax.random.key(seed), 3)
    part_splits = jax.random.split(jax.random.fold_in(key_list[2], part), 3)
    embeddings = draw_embeddings(jax.random.fold_in(jax.random.fold_in(key_list[2], part), 71), part)
    ranks = draw_ranks(jax.random.fold_in(jax.random.fold_in(key_list[2], part), 71), part)
    return {"embeddings": embeddings, "ranks": ranks}


def normalize(embeddings):
    values = embeddings.astype(jnp.float32)
    scale = lax.rsqrt(lax.optimization_barrier(jnp.sum(values * values, axis=1, keepdims=True)) + 1e-06)
    return (values * scale).astype(jnp.bfloat16)

def reference(embeddings, ranks):
    unit = normalize(embeddings)
    row_blocks = unit.reshape(ROWS // ROWS_DEV, ROWS_DEV, D)
    rank_blocks = ranks.reshape(ROWS // ROWS_DEV, ROWS_DEV)

    def one_block(pieces):
        block_rows, block_ranks = pieces
        similar = jnp.dot(block_rows, unit.T, preferred_element_type=jnp.float32)
        earlier = ranks[None, :] < block_ranks[:, None]
        return lax.optimization_barrier(jnp.max(jnp.where(earlier, similar, jnp.float32(-1.0)), axis=1))
    return lax.map(one_block, (row_blocks, rank_blocks)).reshape(ROWS)
```

```python
import jax
import jax.numpy as jnp
from jax import lax
from jax.experimental import pallas as pl
from jax.experimental.pallas import tpu as pltpu
from jax.sharding import PartitionSpec as P

SIZES = (2, 8, 4)
SENDS = [(0, (0, 0, 2)), (0, (0, -2, 0)), (0, (1, 0, 0)), (0, (0, 1, -1)), (1, (1, 0, 0)), (2, (0, 0, -1)), (2, (0, -1, 0)), (3, (0, 1, 0)), (7, (0, 0, -1)), (7, (0, -1, 0))]
ROWS = [6, 8, 2, 5, 1, 4, 3, 7, 9]
STAGES = [[(1, 0), (2, 0), (2, 1), (3, 2), (3, 0), (3, 1), (4, 0), (4, 1), (4, 2), (4, 3), (6, 0), (6, 1), (6, 2), (6, 3), (6, 4), (7, 1), (7, 2), (7, 3), (7, 4), (5, 2), (5, 4), (6, 5), (7, 5)], [(8, 0), (8, 1), (8, 4), (8, 5), (8, 6), (8, 7), (9, 0), (9, 5), (9, 8), (9, 4), (10, 1), (10, 5)]]
BOTH = ("clusters", "members")


def member(coords):
    x, z, y = coords
    return ((x % SIZES[0]) * SIZES[1] + z % SIZES[1]) * SIZES[2] + y % SIZES[2]


def coords_of(index):
    return index // (SIZES[1] * SIZES[2]), (index // SIZES[2]) % SIZES[1], index % SIZES[2]


def mirrored(cluster, shift):
    sign = 1 - 2 * (cluster % 2)
    return shift[0], sign * shift[1], sign * shift[2]


def moved(index, cluster, shift):
    return member(tuple(a + b for a, b in zip(coords_of(index), mirrored(cluster, shift))))


def offsets():
    out = [(0, 0, 0)]
    for slot, shift in SENDS:
        out.append(tuple(a + b for a, b in zip(out[slot], shift)))
    return out


def shift_pairs(shift, back, clusters, members):
    out = []
    for cluster in range(clusters):
        for index in range(members):
            other = cluster * members + moved(index, cluster, shift)
            here = cluster * members + index
            out.append((here, other) if back else (other, here))
    return out


def normalize_kernel(x_ref, out_ref):
    values = x_ref[...].astype(jnp.float32)
    scale = lax.rsqrt(jnp.sum(values * values, axis=1, keepdims=True) + 1e-06)
    out_ref[...] = (values * scale).astype(jnp.bfloat16)


def normalize(embeddings):
    return pl.pallas_call(
        normalize_kernel,
        out_shape=jax.ShapeDtypeStruct(embeddings.shape, jnp.bfloat16),
        in_specs=[pl.BlockSpec(memory_space=pltpu.VMEM)],
        out_specs=pl.BlockSpec(memory_space=pltpu.VMEM),
        compiler_params=pltpu.CompilerParams(vmem_limit_bytes=32 << 20),
        cost_estimate=pl.CostEstimate(flops=4 * embeddings.size, bytes_accessed=4 * embeddings.size, transcendentals=0),
    )(embeddings)


def products(a, b):
    return lax.dot_general(a, b, (((1,), (1,)), ((), ())), preferred_element_type=jnp.float32)


def fold(scores):
    rows, columns = scores.shape
    return jnp.max(scores.reshape(rows // 8, 8, columns), axis=0)


def stage_kernel(slots, pairs, unroll, first, last, *refs):
    count = len(slots)
    order_ref, pairs_ref = refs[0], refs[1]
    blocks = refs[2 : 2 + count]
    refs = refs[2 + count :]
    if first:
        column_ref, row_ref = refs[:2]
        refs = refs[2:]
    else:
        before_ref = refs[0]
        refs = refs[1:]
    out_ref, held, best, sems = refs
    copies = [
        pltpu.make_async_copy(blocks[i], held.at[i], sems.at[i]) for i in range(count)
    ]
    for copy in copies:
        copy.start()
    if first:
        best[...] = jnp.full_like(best, -1.0)
    else:
        best[...] = before_ref[...]
    for copy in copies:
        copy.wait()
    if first:
        own = slots.index(0)
        scores = products(held[own], held[own])
        earlier = column_ref[...] < row_ref[...]
        best[0] = jnp.maximum(best[0], fold(jnp.where(earlier, scores, jnp.float32(-1.0))))

    def step(i, carry):
        for u in range(unroll):
            a = pairs_ref[0, i * unroll + u]
            b = pairs_ref[1, i * unroll + u]
            slot_a = pairs_ref[2, i * unroll + u]
            slot_b = pairs_ref[3, i * unroll + u]
            higher = order_ref[slot_a] > order_ref[slot_b]
            high = jnp.where(higher, a, b)
            low = jnp.where(higher, b, a)
            slot = jnp.where(higher, slot_a, slot_b)
            best[slot] = jnp.maximum(best[slot], fold(products(held[low], held[high])))
        return carry

    lax.fori_loop(0, len(pairs) // unroll, step, 0)
    if last:
        out_ref[...] = jnp.max(best[...], axis=1)
    else:
        out_ref[...] = best[...]


def run_stage(number, order, blocks, ranks, before):
    pairs = STAGES[number]
    first, last = number == 0, number == len(STAGES) - 1
    slots = sorted({s for pair in pairs for s in pair} | ({0} if first else set()))
    unroll = max(u for u in range(1, 6) if len(pairs) % u == 0)
    table = [
        [slots.index(p[0]) for p in pairs],
        [slots.index(p[1]) for p in pairs],
        [p[0] for p in pairs],
        [p[1] for p in pairs],
    ]
    rows, width = blocks[0].shape
    total = len(SENDS) + 1
    smem = pl.BlockSpec(memory_space=pltpu.SMEM)
    vmem = pl.BlockSpec(memory_space=pltpu.VMEM)
    anywhere = pl.BlockSpec(memory_space=pl.ANY)
    if first:
        extra = [ranks.reshape(rows, 1), ranks.reshape(1, rows)]
    else:
        extra = [before]
    shape = (total, rows) if last else (total, 8, rows)

    def kernel(*refs):
        stage_kernel(slots, pairs, unroll, first, last, *refs)

    return pl.pallas_call(
        kernel,
        out_shape=jax.ShapeDtypeStruct(shape, jnp.float32),
        in_specs=[smem, smem] + [anywhere] * len(slots) + [vmem] * len(extra),
        out_specs=vmem,
        scratch_shapes=[
            pltpu.VMEM((len(slots), rows, width), jnp.bfloat16),
            pltpu.VMEM((total, 8, rows), jnp.float32),
            pltpu.SemaphoreType.DMA((len(slots),)),
        ],
        compiler_params=pltpu.CompilerParams(vmem_limit_bytes=32 << 20),
        cost_estimate=pl.CostEstimate(
            flops=2 * rows * rows * width * len(pairs),
            bytes_accessed=2 * rows * width * len(slots),
            transcendentals=0,
        ),
    )(order, jnp.array(table, jnp.int32), *[blocks[s] for s in slots], *extra)


def per_device(clusters, members, embeddings, ranks):
    cluster, index = lax.axis_index("clusters"), lax.axis_index("members")
    places = offsets()
    order = jnp.stack([moved(index, cluster, place) for place in places])
    blocks = [normalize(embeddings)]
    for slot, shift in SENDS:
        blocks.append(lax.ppermute(blocks[slot], BOTH, shift_pairs(shift, False, clusters, members)))
    best = None
    for number in range(len(STAGES)):
        best = run_stage(number, order, blocks, ranks, best)
    result = best[0]
    for slot in ROWS:
        back = lax.ppermute(best[slot], BOTH, shift_pairs(places[slot], True, clusters, members))
        result = jnp.maximum(result, back)
    return result


def solution(mesh):
    clusters, members = mesh.shape["clusters"], mesh.shape["members"]
    in_specs = (P(BOTH, None), P(BOTH))

    def body(embeddings, ranks):
        return per_device(clusters, members, embeddings, ranks)

    return jax.shard_map(body, mesh=mesh, in_specs=in_specs, out_specs=P(BOTH), check_vma=False)
```

```python
import jax
import jax.numpy as jnp
from jax import lax
from jax.experimental import pallas as pl
from jax.experimental.pallas import tpu as pltpu
from jax.sharding import PartitionSpec as P

SIZES = (2, 8, 4)
SENDS = [((0,), (0, -1, 1)), ((0,), (1, 0, 2)), ((0,), (0, 2, 0)), ((0, 1), (0, 0, 1)), ((0, 1), (1, -1, 0)), ((2, 3), (0, 1, 0)), ((1, 3), (0, 0, -1))]
STAGES = [[(1, 0), (2, 0), (2, 1), (3, 0), (3, 1), (3, 2)], [(4, 0), (5, 0), (4, 1), (4, 2), (5, 2), (4, 3), (5, 3)], [(7, 0), (7, 2), (6, 3), (7, 3), (7, 4), (8, 0), (9, 0), (8, 1), (9, 1), (9, 2), (9, 5), (8, 6), (8, 7), (9, 6), (9, 7), (10, 4), (10, 5), (10, 6), (10, 7), (11, 6), (11, 7), (10, 9)]]
BOTH = ("clusters", "members")


def member(coords):
    x, z, y = coords
    return ((x % SIZES[0]) * SIZES[1] + z % SIZES[1]) * SIZES[2] + y % SIZES[2]


def coords_of(index):
    return index // (SIZES[1] * SIZES[2]), (index // SIZES[2]) % SIZES[1], index % SIZES[2]


def mirrored(cluster, shift):
    sign = 1 - 2 * (cluster % 2)
    return shift[0], sign * shift[1], sign * shift[2]


def moved(index, cluster, shift):
    return member(tuple(a + b for a, b in zip(coords_of(index), mirrored(cluster, shift))))


def layout():
    places, homes = [(0, 0, 0)], [(0, 0)]
    for number, (slots, shift) in enumerate(SENDS):
        for place, slot in enumerate(slots):
            places.append(tuple(a + b for a, b in zip(places[slot], shift)))
            homes.append((number + 1, place))
    return places, homes


def shift_pairs(shift, back, clusters, members):
    out = []
    for cluster in range(clusters):
        for index in range(members):
            other = cluster * members + moved(index, cluster, shift)
            here = cluster * members + index
            out.append((here, other) if back else (other, here))
    return out


def normalize_kernel(x_ref, out_ref):
    values = x_ref[...].astype(jnp.float32)
    scale = lax.rsqrt(jnp.sum(values * values, axis=1, keepdims=True) + 1e-06)
    out_ref[...] = (values * scale).astype(jnp.bfloat16)


def normalize(embeddings):
    return pl.pallas_call(
        normalize_kernel,
        out_shape=jax.ShapeDtypeStruct(embeddings.shape, jnp.bfloat16),
        in_specs=[pl.BlockSpec(memory_space=pltpu.VMEM)],
        out_specs=pl.BlockSpec(memory_space=pltpu.VMEM),
        compiler_params=pltpu.CompilerParams(vmem_limit_bytes=32 << 20),
        cost_estimate=pl.CostEstimate(flops=4 * embeddings.size, bytes_accessed=4 * embeddings.size, transcendentals=0),
    )(embeddings)


def products(a, b):
    return lax.dot_general(a, b, (((1,), (1,)), ((), ())), preferred_element_type=jnp.float32)


def fold(scores):
    rows, columns = scores.shape
    return jnp.max(scores.reshape(rows // 8, 8, columns), axis=0)


def stage_kernel(slots, arrays, homes, pairs, first, groups, *refs):
    order_ref, held, refs = refs[0], refs[1 : 1 + len(arrays)], refs[1 + len(arrays) :]
    if first:
        column_ref, row_ref, refs = refs[0], refs[1], refs[2:]
    else:
        before_ref, refs = refs[0], refs[1:]
    outs, blocks, best = refs[:-2], refs[-2], refs[-1]
    for i, slot in enumerate(slots):
        array, place = homes[slot]
        rows = blocks.shape[1]
        blocks[i] = held[arrays.index(array)][pl.ds(place * rows, rows), :]
    if first:
        best[...] = jnp.full_like(best, -1.0)
        own = blocks[slots.index(0)]
        earlier = column_ref[...] < row_ref[...]
        best[0] = fold(jnp.where(earlier, products(own, own), jnp.float32(-1.0)))
    else:
        best[...] = before_ref[...]
    for a, b in pairs:
        higher = order_ref[a] > order_ref[b]
        i, j = slots.index(a), slots.index(b)
        high, low = jnp.where(higher, i, j), jnp.where(higher, j, i)
        slot = jnp.where(higher, a, b)
        best[slot] = jnp.maximum(best[slot], fold(products(blocks[low], blocks[high])))
    if groups is None:
        outs[0][...] = best[...]
    else:
        for out, (start, stop) in zip(outs, groups):
            out[...] = jnp.max(best[start:stop], axis=1)


def run_stage(number, order, arrays, homes, ranks, before, groups):
    pairs = STAGES[number]
    first, last = number == 0, number == len(STAGES) - 1
    slots = sorted({s for pair in pairs for s in pair} | ({0} if first else set()))
    needed = sorted({homes[s][0] for s in slots})
    rows, width = arrays[0].shape
    total = len(homes)
    smem = pl.BlockSpec(memory_space=pltpu.SMEM)
    vmem = pl.BlockSpec(memory_space=pltpu.VMEM)
    if first:
        extra = [ranks.reshape(rows, 1), ranks.reshape(1, rows)]
    else:
        extra = [before]
    if last:
        shapes = [jax.ShapeDtypeStruct((stop - start, rows), jnp.float32) for start, stop in groups]
    else:
        shapes = [jax.ShapeDtypeStruct((total, 8, rows), jnp.float32)]

    def kernel(*refs):
        stage_kernel(slots, needed, homes, pairs, first, groups if last else None, *refs)

    out = pl.pallas_call(
        kernel,
        out_shape=shapes,
        in_specs=[smem] + [vmem] * (len(needed) + len(extra)),
        out_specs=[vmem] * len(shapes),
        scratch_shapes=[
            pltpu.VMEM((len(slots), rows, width), jnp.bfloat16),
            pltpu.VMEM((total, 8, rows), jnp.float32),
        ],
        compiler_params=pltpu.CompilerParams(vmem_limit_bytes=32 << 20),
        cost_estimate=pl.CostEstimate(
            flops=2 * rows * rows * width * len(pairs),
            bytes_accessed=2 * rows * width * len(slots),
            transcendentals=0,
        ),
    )(order, *[arrays[n] for n in needed], *extra)
    return out if last else out[0]


def per_device(clusters, members, embeddings, ranks):
    cluster, index = lax.axis_index("clusters"), lax.axis_index("members")
    places, homes = layout()
    order = jnp.stack([moved(index, cluster, place) for place in places])
    rows = embeddings.shape[0]
    arrays = [normalize(embeddings)]

    def block(slot):
        array, place = homes[slot]
        return arrays[array][place * rows : (place + 1) * rows]

    for slots, shift in SENDS:
        blocks = [block(slot) for slot in slots]
        stack = blocks[0] if len(blocks) == 1 else jnp.concatenate(blocks, axis=0)
        arrays.append(lax.ppermute(stack, BOTH, shift_pairs(shift, False, clusters, members)))
    bounds, start = [(0, 1)], 1
    for slots, _ in SENDS:
        bounds.append((start, start + len(slots)))
        start += len(slots)
    best = None
    for number in range(len(STAGES)):
        best = run_stage(number, order, arrays, homes, ranks, best, bounds)
    best = list(best)
    for number in reversed(range(len(SENDS))):
        slots, shift = SENDS[number]
        back = lax.ppermute(best[number + 1], BOTH, shift_pairs(shift, True, clusters, members))
        for place, slot in enumerate(slots):
            array, at = homes[slot]
            row = jnp.maximum(best[array][at], back[place])
            best[array] = row[None] if best[array].shape[0] == 1 else best[array].at[at].set(row)
    return best[0][0]


def solution(mesh):
    clusters, members = mesh.shape["clusters"], mesh.shape["members"]
    in_specs = (P(BOTH, None), P(BOTH))

    def body(embeddings, ranks):
        return per_device(clusters, members, embeddings, ranks)

    return jax.shard_map(body, mesh=mesh, in_specs=in_specs, out_specs=P(BOTH), check_vma=False)
```

```python
import jax
import jax.numpy as jnp
from jax import lax
from jax.experimental import pallas as pl
from jax.experimental.pallas import tpu as pltpu
from jax.sharding import PartitionSpec as P

SIZES = (2, 8, 4)
SENDS = [((0,), (0, 0, 2)), ((0,), (0, -2, 0)), ((0,), (1, 0, 0)), ((0,), (0, 1, -1)), ((1,), (1, 0, 0)), ((2,), (0, 0, -1)), ((2,), (0, -1, 0)), ((3,), (0, 1, 0)), ((7,), (0, 0, -1)), ((7,), (0, -1, 0))]
STAGES = [[(2, 0), (1, 0), (2, 1), (3, 0), (3, 2), (3, 1)], [(7, 0), (7, 2), (7, 1), (7, 3), (4, 0), (4, 2), (4, 1), (4, 3), (7, 4), (5, 2), (7, 5), (5, 4), (8, 0), (8, 1), (8, 7), (8, 4), (8, 5), (6, 0), (6, 2), (6, 1), (6, 3), (6, 5), (8, 6)], [(10, 0), (10, 1), (10, 4), (10, 5), (9, 5), (9, 8)]]
BOTH = ("clusters", "members")


def member(coords):
    x, z, y = coords
    return ((x % SIZES[0]) * SIZES[1] + z % SIZES[1]) * SIZES[2] + y % SIZES[2]


def coords_of(index):
    return index // (SIZES[1] * SIZES[2]), (index // SIZES[2]) % SIZES[1], index % SIZES[2]


def mirrored(cluster, shift):
    sign = 1 - 2 * (cluster % 2)
    return shift[0], sign * shift[1], sign * shift[2]


def moved(index, cluster, shift):
    return member(tuple(a + b for a, b in zip(coords_of(index), mirrored(cluster, shift))))


def layout():
    places, homes = [(0, 0, 0)], [(0, 0)]
    for number, (slots, shift) in enumerate(SENDS):
        for place, slot in enumerate(slots):
            places.append(tuple(a + b for a, b in zip(places[slot], shift)))
            homes.append((number + 1, place))
    return places, homes


def shift_pairs(shift, back, clusters, members):
    out = []
    for cluster in range(clusters):
        for index in range(members):
            other = cluster * members + moved(index, cluster, shift)
            here = cluster * members + index
            out.append((here, other) if back else (other, here))
    return out


def normalize_kernel(x_ref, out_ref):
    values = x_ref[...].astype(jnp.float32)
    scale = lax.rsqrt(jnp.sum(values * values, axis=1, keepdims=True) + 1e-06)
    out_ref[...] = (values * scale).astype(jnp.bfloat16)


def normalize(embeddings):
    return pl.pallas_call(
        normalize_kernel,
        out_shape=jax.ShapeDtypeStruct(embeddings.shape, jnp.bfloat16),
        in_specs=[pl.BlockSpec(memory_space=pltpu.VMEM)],
        out_specs=pl.BlockSpec(memory_space=pltpu.VMEM),
        compiler_params=pltpu.CompilerParams(vmem_limit_bytes=32 << 20),
        cost_estimate=pl.CostEstimate(flops=4 * embeddings.size, bytes_accessed=4 * embeddings.size, transcendentals=0),
    )(embeddings)


def products(a, b):
    return lax.dot_general(a, b, (((1,), (1,)), ((), ())), preferred_element_type=jnp.float32)


def fold(scores):
    rows, columns = scores.shape
    return jnp.max(scores.reshape(rows // 8, 8, columns), axis=0)


def stage_kernel(slots, arrays, homes, pairs, first, groups, *refs):
    order_ref, held, refs = refs[0], refs[1 : 1 + len(arrays)], refs[1 + len(arrays) :]
    if first:
        column_ref, row_ref, refs = refs[0], refs[1], refs[2:]
    else:
        before_ref, refs = refs[0], refs[1:]
    outs, blocks, best = refs[:-2], refs[-2], refs[-1]
    for i, slot in enumerate(slots):
        array, place = homes[slot]
        rows = blocks.shape[1]
        blocks[i] = held[arrays.index(array)][pl.ds(place * rows, rows), :]
    if first:
        best[...] = jnp.full_like(best, -1.0)
        own = blocks[slots.index(0)]
        earlier = column_ref[...] < row_ref[...]
        best[0] = fold(jnp.where(earlier, products(own, own), jnp.float32(-1.0)))
    else:
        best[...] = before_ref[...]
    for a, b in pairs:
        higher = order_ref[a] > order_ref[b]
        i, j = slots.index(a), slots.index(b)
        high, low = jnp.where(higher, i, j), jnp.where(higher, j, i)
        slot = jnp.where(higher, a, b)
        best[slot] = jnp.maximum(best[slot], fold(products(blocks[low], blocks[high])))
    if groups is None:
        outs[0][...] = best[...]
    else:
        out = outs[0]
        out[...] = jnp.full_like(out, -1.0)
        for slot in range(best.shape[0]):
            out[pl.ds(order_ref[slot], 1), :] = jnp.max(best[slot], axis=0, keepdims=True)


def run_stage(number, order, arrays, homes, ranks, before, groups):
    pairs = STAGES[number]
    first, last = number == 0, number == len(STAGES) - 1
    slots = sorted({s for pair in pairs for s in pair} | ({0} if first else set()))
    needed = sorted({homes[s][0] for s in slots})
    rows, width = arrays[0].shape
    total = len(homes)
    smem = pl.BlockSpec(memory_space=pltpu.SMEM)
    vmem = pl.BlockSpec(memory_space=pltpu.VMEM)
    if first:
        extra = [ranks.reshape(rows, 1), ranks.reshape(1, rows)]
    else:
        extra = [before]
    if last:
        shapes = [jax.ShapeDtypeStruct((groups, rows), jnp.float32)]
    else:
        shapes = [jax.ShapeDtypeStruct((total, 8, rows), jnp.float32)]

    def kernel(*refs):
        stage_kernel(slots, needed, homes, pairs, first, groups if last else None, *refs)

    out = pl.pallas_call(
        kernel,
        out_shape=shapes,
        in_specs=[smem] + [vmem] * (len(needed) + len(extra)),
        out_specs=[vmem] * len(shapes),
        scratch_shapes=[
            pltpu.VMEM((len(slots), rows, width), jnp.bfloat16),
            pltpu.VMEM((total, 8, rows), jnp.float32),
        ],
        compiler_params=pltpu.CompilerParams(vmem_limit_bytes=32 << 20),
        cost_estimate=pl.CostEstimate(
            flops=2 * rows * rows * width * len(pairs),
            bytes_accessed=2 * rows * width * len(slots),
            transcendentals=0,
        ),
    )(order, *[arrays[n] for n in needed], *extra)
    return out[0]


def per_device(clusters, members, embeddings, ranks):
    cluster, index = lax.axis_index("clusters"), lax.axis_index("members")
    places, homes = layout()
    order = jnp.stack([moved(index, cluster, place) for place in places])
    rows = embeddings.shape[0]
    arrays = [normalize(embeddings)]

    def block(slot):
        array, place = homes[slot]
        return arrays[array][place * rows : (place + 1) * rows]

    for slots, shift in SENDS:
        blocks = [block(slot) for slot in slots]
        stack = blocks[0] if len(blocks) == 1 else jnp.concatenate(blocks, axis=0)
        arrays.append(lax.ppermute(stack, BOTH, shift_pairs(shift, False, clusters, members)))
    best = None
    for number in range(len(STAGES)):
        best = run_stage(number, order, arrays, homes, ranks, best, members)
    found = lax.all_to_all(best, "members", 0, 0, tiled=True)
    return jnp.max(found, axis=0)


def solution(mesh):
    clusters, members = mesh.shape["clusters"], mesh.shape["members"]
    in_specs = (P(BOTH, None), P(BOTH))

    def body(embeddings, ranks):
        return per_device(clusters, members, embeddings, ranks)

    return jax.shard_map(body, mesh=mesh, in_specs=in_specs, out_specs=P(BOTH), check_vma=False)
```

```python
import jax
import jax.numpy as jnp
from jax import lax
from jax.experimental import pallas as pl
from jax.experimental.pallas import tpu as pltpu
from jax.sharding import PartitionSpec as P

SIZES = (2, 8, 4)
SENDS = [((0,), (0, 0, 2)), ((0,), (0, -2, 0)), ((0,), (1, 0, 0)), ((0,), (0, 1, -1)), ((1,), (1, 0, 0)), ((2,), (0, 0, -1)), ((2,), (0, -1, 0)), ((3,), (0, 1, 0)), ((7,), (0, 0, -1)), ((7,), (0, -1, 0))]
STAGES = [([(1, 0), (2, 0), (2, 1), (3, 0), (3, 1), (3, 2)], []), ([(7, 6), (4, 1), (4, 2), (4, 3), (5, 2), (5, 4), (6, 0), (6, 1), (6, 2), (6, 3), (7, 0), (6, 5), (7, 1), (8, 3), (8, 2), (7, 4), (7, 5), (8, 0), (8, 1), (8, 4), (8, 5), (8, 6), (8, 7)], [2, 3, 4, 6, 7]), ([(9, 0), (10, 0), (9, 5), (9, 8), (10, 1), (10, 5)], [1, 5, 8, 9])]
BOTH = ("clusters", "members")


def member(coords):
    x, z, y = coords
    return ((x % SIZES[0]) * SIZES[1] + z % SIZES[1]) * SIZES[2] + y % SIZES[2]


def coords_of(index):
    return index // (SIZES[1] * SIZES[2]), (index // SIZES[2]) % SIZES[1], index % SIZES[2]


def mirrored(cluster, shift):
    sign = 1 - 2 * (cluster % 2)
    return shift[0], sign * shift[1], sign * shift[2]


def moved(index, cluster, shift):
    return member(tuple(a + b for a, b in zip(coords_of(index), mirrored(cluster, shift))))


def layout():
    places, homes = [(0, 0, 0)], [(0, 0)]
    for number, (slots, shift) in enumerate(SENDS):
        for place, slot in enumerate(slots):
            places.append(tuple(a + b for a, b in zip(places[slot], shift)))
            homes.append((number + 1, place))
    return places, homes


def shift_pairs(shift, back, clusters, members):
    out = []
    for cluster in range(clusters):
        for index in range(members):
            other = cluster * members + moved(index, cluster, shift)
            here = cluster * members + index
            out.append((here, other) if back else (other, here))
    return out


def normalize_kernel(x_ref, out_ref):
    values = x_ref[...].astype(jnp.float32)
    scale = lax.rsqrt(jnp.sum(values * values, axis=1, keepdims=True) + 1e-06)
    out_ref[...] = (values * scale).astype(jnp.bfloat16)


def normalize(embeddings):
    return pl.pallas_call(
        normalize_kernel,
        out_shape=jax.ShapeDtypeStruct(embeddings.shape, jnp.bfloat16),
        in_specs=[pl.BlockSpec(memory_space=pltpu.VMEM)],
        out_specs=pl.BlockSpec(memory_space=pltpu.VMEM),
        compiler_params=pltpu.CompilerParams(vmem_limit_bytes=32 << 20),
        cost_estimate=pl.CostEstimate(flops=4 * embeddings.size, bytes_accessed=4 * embeddings.size, transcendentals=0),
    )(embeddings)


def products(a, b):
    return lax.dot_general(a, b, (((1,), (1,)), ((), ())), preferred_element_type=jnp.float32)


def fold(scores):
    rows, columns = scores.shape
    return jnp.max(scores.reshape(rows // 8, 8, columns), axis=0)


def stage_kernel(slots, arrays, homes, stage, back, *refs):
    pairs, done = STAGES[stage]
    first, last = stage == 0, stage == len(STAGES) - 1
    order_ref, held, refs = refs[0], refs[1 : 1 + len(arrays)], refs[1 + len(arrays) :]
    if first:
        column_ref, row_ref, refs = refs[0], refs[1], refs[2:]
    else:
        before_ref, refs = refs[0], refs[1:]
    backs, refs = refs[:back], refs[back:]
    outs, blocks, best = refs[:-2], refs[-2], refs[-1]
    for i, slot in enumerate(slots):
        array, place = homes[slot]
        rows = blocks.shape[1]
        blocks[i] = held[arrays.index(array)][pl.ds(place * rows, rows), :]
    if first:
        best[...] = jnp.full_like(best, -1.0)
        own = blocks[slots.index(0)]
        earlier = column_ref[...] < row_ref[...]
        best[0] = fold(jnp.where(earlier, products(own, own), jnp.float32(-1.0)))
    else:
        best[...] = before_ref[...]
    for ref in backs:
        best[0] = jnp.maximum(best[0], ref[...])
    for a, b in pairs:
        higher = order_ref[a] > order_ref[b]
        i, j = slots.index(a), slots.index(b)
        high, low = jnp.where(higher, i, j), jnp.where(higher, j, i)
        slot = jnp.where(higher, a, b)
        best[slot] = jnp.maximum(best[slot], fold(products(blocks[low], blocks[high])))
    if not last:
        outs[0][...] = best[...]
    for out, slot in zip(outs if last else outs[1:], [0] * last + list(done)):
        out[...] = jnp.max(best[slot], axis=0, keepdims=True)


def run_stage(stage, order, arrays, homes, ranks, before, backs):
    pairs, done = STAGES[stage]
    first, last = stage == 0, stage == len(STAGES) - 1
    slots = sorted({s for pair in pairs for s in pair} | ({0} if first else set()))
    needed = sorted({homes[s][0] for s in slots})
    rows, width = arrays[0].shape
    total = len(homes)
    smem = pl.BlockSpec(memory_space=pltpu.SMEM)
    vmem = pl.BlockSpec(memory_space=pltpu.VMEM)
    if first:
        extra = [ranks.reshape(rows, 1), ranks.reshape(1, rows)]
    else:
        extra = [before] + backs
    shapes = [] if last else [jax.ShapeDtypeStruct((total, 8, rows), jnp.float32)]
    shapes += [jax.ShapeDtypeStruct((1, rows), jnp.float32)] * (len(done) + last)

    def kernel(*refs):
        stage_kernel(slots, needed, homes, stage, len(backs), *refs)

    return pl.pallas_call(
        kernel,
        out_shape=shapes,
        in_specs=[smem] + [vmem] * (len(needed) + len(extra)),
        out_specs=[vmem] * len(shapes),
        scratch_shapes=[
            pltpu.VMEM((len(slots), rows, width), jnp.bfloat16),
            pltpu.VMEM((total, 8, rows), jnp.float32),
        ],
        compiler_params=pltpu.CompilerParams(vmem_limit_bytes=32 << 20),
        cost_estimate=pl.CostEstimate(
            flops=2 * rows * rows * width * len(pairs),
            bytes_accessed=2 * rows * width * len(slots),
            transcendentals=0,
        ),
    )(order, *[arrays[n] for n in needed], *extra)


def per_device(clusters, members, embeddings, ranks):
    cluster, index = lax.axis_index("clusters"), lax.axis_index("members")
    places, homes = layout()
    order = jnp.stack([moved(index, cluster, place) for place in places])
    rows = embeddings.shape[0]
    arrays = [normalize(embeddings)]

    def block(slot):
        array, place = homes[slot]
        return arrays[array][place * rows : (place + 1) * rows]

    for slots, shift in SENDS:
        blocks = [block(slot) for slot in slots]
        stack = blocks[0] if len(blocks) == 1 else jnp.concatenate(blocks, axis=0)
        arrays.append(lax.ppermute(stack, BOTH, shift_pairs(shift, False, clusters, members)))
    best, backs = None, []
    for stage, (_, done) in enumerate(STAGES):
        best, *rest = run_stage(stage, order, arrays, homes, ranks, best, backs)
        backs = [
            lax.ppermute(row, BOTH, shift_pairs(places[slot], True, clusters, members))
            for row, slot in zip(rest, done)
        ]
    for back in backs:
        best = jnp.maximum(best, back)
    return best[0]


def solution(mesh):
    clusters, members = mesh.shape["clusters"], mesh.shape["members"]
    in_specs = (P(BOTH, None), P(BOTH))

    def body(embeddings, ranks):
        return per_device(clusters, members, embeddings, ranks)

    return jax.shard_map(body, mesh=mesh, in_specs=in_specs, out_specs=P(BOTH), check_vma=False)
```

```python
import jax
import jax.numpy as jnp
from jax import lax
from jax.experimental import pallas as pl
from jax.experimental.pallas import tpu as pltpu
from jax.sharding import PartitionSpec as P

SIZES = (2, 8, 4)
SENDS = [((0,), (0, 0, -1)), ((0,), (0, 2, 0)), ((0,), (1, 0, 1)), ((1,), (0, 0, -1)), ((0,), (0, 1, 1)), ((2,), (0, 1, 0)), ((1,), (1, 0, 0)), ((3,), (0, 0, 1)), ((3,), (0, 0, -1)), ((6,), (0, 1, 0))]
STAGES = [[(1, 0), (2, 0), (2, 1), (3, 0), (3, 1), (3, 2), (5, 0), (5, 1), (5, 2), (5, 3)], [(9, 8), (6, 0), (6, 1), (6, 2), (6, 3), (6, 5), (7, 1), (7, 2), (7, 5), (7, 6), (8, 2), (8, 5), (8, 6), (9, 2), (9, 5), (9, 6)], [(4, 2), (6, 4), (10, 0), (10, 1), (10, 3), (10, 4), (10, 5), (10, 8), (10, 9)]]
BOTH = ("clusters", "members")


def member(coords):
    x, z, y = coords
    return ((x % SIZES[0]) * SIZES[1] + z % SIZES[1]) * SIZES[2] + y % SIZES[2]


def coords_of(index):
    return index // (SIZES[1] * SIZES[2]), (index // SIZES[2]) % SIZES[1], index % SIZES[2]


def mirrored(cluster, shift):
    sign = 1 - 2 * (cluster % 2)
    return shift[0], sign * shift[1], sign * shift[2]


def moved(index, cluster, shift):
    return member(tuple(a + b for a, b in zip(coords_of(index), mirrored(cluster, shift))))


def layout():
    places, homes = [(0, 0, 0)], [(0, 0)]
    for number, (slots, shift) in enumerate(SENDS):
        for place, slot in enumerate(slots):
            places.append(tuple(a + b for a, b in zip(places[slot], shift)))
            homes.append((number + 1, place))
    return places, homes


def shift_pairs(shift, back, clusters, members):
    out = []
    for cluster in range(clusters):
        for index in range(members):
            other = cluster * members + moved(index, cluster, shift)
            here = cluster * members + index
            out.append((here, other) if back else (other, here))
    return out


def normalize_kernel(x_ref, out_ref):
    values = x_ref[...].astype(jnp.float32)
    scale = lax.rsqrt(jnp.sum(values * values, axis=1, keepdims=True) + 1e-06)
    out_ref[...] = (values * scale).astype(jnp.bfloat16)


def normalize(embeddings):
    return pl.pallas_call(
        normalize_kernel,
        out_shape=jax.ShapeDtypeStruct(embeddings.shape, jnp.bfloat16),
        in_specs=[pl.BlockSpec(memory_space=pltpu.VMEM)],
        out_specs=pl.BlockSpec(memory_space=pltpu.VMEM),
        compiler_params=pltpu.CompilerParams(vmem_limit_bytes=32 << 20),
        cost_estimate=pl.CostEstimate(flops=4 * embeddings.size, bytes_accessed=4 * embeddings.size, transcendentals=0),
    )(embeddings)


def products(a, b):
    return lax.dot_general(a, b, (((1,), (1,)), ((), ())), preferred_element_type=jnp.float32)


def fold(scores):
    rows, columns = scores.shape
    return jnp.max(scores.reshape(rows // 8, 8, columns), axis=0)


def stage_kernel(slots, arrays, homes, pairs, first, groups, *refs):
    order_ref, held, refs = refs[0], refs[1 : 1 + len(arrays)], refs[1 + len(arrays) :]
    if first:
        column_ref, row_ref, refs = refs[0], refs[1], refs[2:]
    else:
        before_ref, refs = refs[0], refs[1:]
    outs, blocks, best = refs[:-2], refs[-2], refs[-1]
    for i, slot in enumerate(slots):
        array, place = homes[slot]
        rows = blocks.shape[1]
        blocks[i] = held[arrays.index(array)][pl.ds(place * rows, rows), :]
    if first:
        best[...] = jnp.full_like(best, -1.0)
        own = blocks[slots.index(0)]
        earlier = column_ref[...] < row_ref[...]
        best[0] = fold(jnp.where(earlier, products(own, own), jnp.float32(-1.0)))
    else:
        best[...] = before_ref[...]
    for a, b in pairs:
        higher = order_ref[a] > order_ref[b]
        i, j = slots.index(a), slots.index(b)
        high, low = jnp.where(higher, i, j), jnp.where(higher, j, i)
        slot = jnp.where(higher, a, b)
        best[slot] = jnp.maximum(best[slot], fold(products(blocks[low], blocks[high])))
    if groups is None:
        outs[0][...] = best[...]
    else:
        out = outs[0]
        out[...] = jnp.full_like(out, -1.0)
        for slot in range(best.shape[0]):
            out[pl.ds(order_ref[slot], 1), :] = jnp.max(best[slot], axis=0, keepdims=True)


def run_stage(number, order, arrays, homes, ranks, before, groups):
    pairs = STAGES[number]
    first, last = number == 0, number == len(STAGES) - 1
    slots = sorted({s for pair in pairs for s in pair} | ({0} if first else set()))
    needed = sorted({homes[s][0] for s in slots})
    rows, width = arrays[0].shape
    total = len(homes)
    smem = pl.BlockSpec(memory_space=pltpu.SMEM)
    vmem = pl.BlockSpec(memory_space=pltpu.VMEM)
    if first:
        extra = [ranks.reshape(rows, 1), ranks.reshape(1, rows)]
    else:
        extra = [before]
    if last:
        shapes = [jax.ShapeDtypeStruct((groups, rows), jnp.float32)]
    else:
        shapes = [jax.ShapeDtypeStruct((total, 8, rows), jnp.float32)]

    def kernel(*refs):
        stage_kernel(slots, needed, homes, pairs, first, groups if last else None, *refs)

    out = pl.pallas_call(
        kernel,
        out_shape=shapes,
        in_specs=[smem] + [vmem] * (len(needed) + len(extra)),
        out_specs=[vmem] * len(shapes),
        scratch_shapes=[
            pltpu.VMEM((len(slots), rows, width), jnp.bfloat16),
            pltpu.VMEM((total, 8, rows), jnp.float32),
        ],
        compiler_params=pltpu.CompilerParams(vmem_limit_bytes=32 << 20),
        cost_estimate=pl.CostEstimate(
            flops=2 * rows * rows * width * len(pairs),
            bytes_accessed=2 * rows * width * len(slots),
            transcendentals=0,
        ),
    )(order, *[arrays[n] for n in needed], *extra)
    return out[0]


def per_device(clusters, members, embeddings, ranks):
    cluster, index = lax.axis_index("clusters"), lax.axis_index("members")
    places, homes = layout()
    order = jnp.stack([moved(index, cluster, place) for place in places])
    rows = embeddings.shape[0]
    arrays = [normalize(embeddings)]

    def block(slot):
        array, place = homes[slot]
        return arrays[array][place * rows : (place + 1) * rows]

    for slots, shift in SENDS:
        blocks = [block(slot) for slot in slots]
        stack = blocks[0] if len(blocks) == 1 else jnp.concatenate(blocks, axis=0)
        arrays.append(lax.ppermute(stack, BOTH, shift_pairs(shift, False, clusters, members)))
    best = None
    for number in range(len(STAGES)):
        best = run_stage(number, order, arrays, homes, ranks, best, members)
    found = lax.all_to_all(best, "members", 0, 0, tiled=True)
    return jnp.max(found, axis=0)


def solution(mesh):
    clusters, members = mesh.shape["clusters"], mesh.shape["members"]
    in_specs = (P(BOTH, None), P(BOTH))

    def body(embeddings, ranks):
        return per_device(clusters, members, embeddings, ranks)

    return jax.shard_map(body, mesh=mesh, in_specs=in_specs, out_specs=P(BOTH), check_vma=False)
```

```python
import jax
import jax.numpy as jnp
from jax import lax
from jax.experimental import pallas as pl
from jax.experimental.pallas import tpu as pltpu
from jax.sharding import PartitionSpec as P

SIZES = (2, 8, 4)
SENDS = [((0,), (0, 0, -1)), ((0,), (0, 2, 0)), ((0,), (1, 0, 1)), ((0,), (0, 1, 1)), ((1,), (0, 0, -1)), ((2,), (0, 1, 0)), ((1,), (1, 0, 0)), ((3,), (0, 0, 1)), ((3,), (0, 0, -1)), ((6,), (0, 1, 0))]
STAGES = [[(2, 0), (3, 0), (3, 2)], [(1, 0), (2, 1), (3, 1), (4, 0), (4, 1), (4, 2), (4, 3)], [(9, 8), (6, 0), (6, 1), (6, 2), (6, 3), (6, 4), (9, 0), (8, 2), (8, 4), (8, 6), (9, 2), (9, 4), (9, 6)], [(5, 2), (6, 5), (7, 2), (7, 4), (7, 6)], [(10, 0), (10, 1), (10, 7), (10, 4), (10, 5), (10, 8), (10, 9)]]
FIRST = 5
HELD = (2, 1)
BOTH = ("clusters", "members")


def member(coords):
    x, z, y = coords
    return ((x % SIZES[0]) * SIZES[1] + z % SIZES[1]) * SIZES[2] + y % SIZES[2]


def coords_of(index):
    return index // (SIZES[1] * SIZES[2]), (index // SIZES[2]) % SIZES[1], index % SIZES[2]


def mirrored(cluster, shift):
    sign = 1 - 2 * (cluster % 2)
    return shift[0], sign * shift[1], sign * shift[2]


def moved(index, cluster, shift):
    return member(tuple(a + b for a, b in zip(coords_of(index), mirrored(cluster, shift))))


def layout():
    places, homes = [(0, 0, 0)], [(0, 0)]
    for number, (slots, shift) in enumerate(SENDS):
        for place, slot in enumerate(slots):
            places.append(tuple(a + b for a, b in zip(places[slot], shift)))
            homes.append((number + 1, place))
    return places, homes


def shift_pairs(shift, back, clusters, members):
    out = []
    for cluster in range(clusters):
        for index in range(members):
            other = cluster * members + moved(index, cluster, shift)
            here = cluster * members + index
            out.append((here, other) if back else (other, here))
    return out


def normalize_kernel(x_ref, out_ref):
    values = x_ref[...].astype(jnp.float32)
    scale = lax.rsqrt(jnp.sum(values * values, axis=1, keepdims=True) + 1e-06)
    out_ref[...] = (values * scale).astype(jnp.bfloat16)


def normalize(embeddings):
    return pl.pallas_call(
        normalize_kernel,
        out_shape=jax.ShapeDtypeStruct(embeddings.shape, jnp.bfloat16),
        in_specs=[pl.BlockSpec(memory_space=pltpu.VMEM)],
        out_specs=pl.BlockSpec(memory_space=pltpu.VMEM),
        compiler_params=pltpu.CompilerParams(vmem_limit_bytes=32 << 20),
        cost_estimate=pl.CostEstimate(flops=4 * embeddings.size, bytes_accessed=4 * embeddings.size, transcendentals=0),
    )(embeddings)


def products(a, b):
    return lax.dot_general(a, b, (((1,), (1,)), ((), ())), preferred_element_type=jnp.float32)


def fold(scores):
    rows, columns = scores.shape
    return jnp.max(scores.reshape(rows // 8, 8, columns), axis=0)


def own_kernel(unit_ref, column_ref, row_ref, best_ref):
    best_ref[...] = jnp.full_like(best_ref, -1.0)
    earlier = column_ref[...] < row_ref[...]
    scores = products(unit_ref[...], unit_ref[...])
    best_ref[0] = fold(jnp.where(earlier, scores, jnp.float32(-1.0)))


def stage_kernel(slots, pairs, last, *refs):
    count = len(slots)
    order_ref, blocks, before_ref = refs[0], refs[1 : 1 + count], refs[1 + count]
    out, best = refs[2 + count :]
    best[...] = before_ref[...]
    for a, b in pairs:
        higher = order_ref[a] > order_ref[b]
        scores = products(blocks[slots.index(a)][...], blocks[slots.index(b)][...])
        best[b] = jnp.where(higher, best[b], jnp.maximum(best[b], fold(scores)))
        best[a] = jnp.where(higher, jnp.maximum(best[a], jnp.max(scores, axis=1)[None, :]), best[a])
    if last:
        out[...] = jnp.full_like(out, -1.0)
        for slot in range(best.shape[0]):
            out[pl.ds(order_ref[slot], 1), :] = jnp.max(best[slot], axis=0, keepdims=True)
    else:
        out[...] = best[...]


def call_kernel(kernel, shape, specs, scratch, products_done, *args):
    rows, width = 256, 768
    return pl.pallas_call(
        kernel,
        out_shape=jax.ShapeDtypeStruct(shape, jnp.float32),
        in_specs=specs,
        out_specs=pl.BlockSpec(memory_space=pltpu.VMEM),
        scratch_shapes=scratch,
        compiler_params=pltpu.CompilerParams(vmem_limit_bytes=32 << 20),
        cost_estimate=pl.CostEstimate(
            flops=2 * rows * rows * width * products_done,
            bytes_accessed=2 * rows * width * products_done,
            transcendentals=0,
        ),
    )(*args)


def per_device(clusters, members, embeddings, ranks):
    cluster, index = lax.axis_index("clusters"), lax.axis_index("members")
    places, _ = layout()
    order = jnp.stack([moved(index, cluster, place) for place in places])
    rows = embeddings.shape[0]
    total = len(places)
    smem = pl.BlockSpec(memory_space=pltpu.SMEM)
    vmem = pl.BlockSpec(memory_space=pltpu.VMEM)
    blocks = [normalize(embeddings)]
    best = call_kernel(
        own_kernel, (total, 8, rows), [vmem] * 3, [], 1, blocks[0], ranks.reshape(rows, 1), ranks.reshape(1, rows)
    )

    def compare(stage, best):
        pairs, last = STAGES[stage], stage == len(STAGES) - 1
        slots = sorted({s for pair in pairs for s in pair})

        def kernel(*refs):
            stage_kernel(slots, pairs, last, *refs)

        return call_kernel(
            kernel,
            (members, rows) if last else (total, 8, rows),
            [smem] + [vmem] * (len(slots) + 1),
            [pltpu.VMEM((total, 8, rows), jnp.float32)],
            len(pairs),
            order,
            *[blocks[s] for s in slots],
            best,
        )

    for (slot,), shift in SENDS:
        if slot and len(blocks) == FIRST:
            blocks[HELD[0]], best, order = lax.optimization_barrier((blocks[HELD[0]], best, order))
            best = compare(0, best)
            blocks[HELD[1]], best = lax.optimization_barrier((blocks[HELD[1]], best))
        blocks.append(lax.ppermute(blocks[slot], BOTH, shift_pairs(shift, False, clusters, members)))
    for stage in range(1, len(STAGES)):
        best = compare(stage, best)
    found = lax.all_to_all(best, "members", 0, 0, tiled=True)
    return jnp.max(found, axis=0)


def solution(mesh):
    clusters, members = mesh.shape["clusters"], mesh.shape["members"]
    in_specs = (P(BOTH, None), P(BOTH))

    def body(embeddings, ranks):
        return per_device(clusters, members, embeddings, ranks)

    return jax.shard_map(body, mesh=mesh, in_specs=in_specs, out_specs=P(BOTH), check_vma=False)
```

```python
import jax
import jax.numpy as jnp
from jax import lax
from jax.experimental import pallas as pl
from jax.experimental.pallas import tpu as pltpu
from jax.sharding import PartitionSpec as P

SIZES = (2, 8, 4)
SENDS = [((0,), (0, 0, -1)), ((0,), (0, 2, 0)), ((0,), (1, 0, 1)), ((0,), (0, 1, 1)), ((1,), (0, 0, -1)), ((2,), (0, 1, 0)), ((1,), (1, 0, 0)), ((3,), (0, 0, 1)), ((3,), (0, 0, -1)), ((6,), (0, 1, 0))]
STAGES = [[(2, 0), (3, 0), (3, 2)], [(1, 0), (2, 1), (3, 1), (4, 0), (4, 1), (4, 2), (4, 3)], [(9, 8), (6, 0), (6, 1), (6, 2), (6, 3), (6, 4), (9, 0), (8, 2), (8, 4), (8, 6), (9, 2), (9, 4), (9, 6)], [(5, 2), (6, 5), (7, 2), (7, 4), (7, 6), (10, 0), (10, 1), (10, 7), (10, 4), (10, 5), (10, 8), (10, 9)]]
FIRST = 5
HELD = (2, 1)
BOTH = ("clusters", "members")


def member(coords):
    x, z, y = coords
    return ((x % SIZES[0]) * SIZES[1] + z % SIZES[1]) * SIZES[2] + y % SIZES[2]


def coords_of(index):
    return index // (SIZES[1] * SIZES[2]), (index // SIZES[2]) % SIZES[1], index % SIZES[2]


def mirrored(cluster, shift):
    sign = 1 - 2 * (cluster % 2)
    return shift[0], sign * shift[1], sign * shift[2]


def moved(index, cluster, shift):
    return member(tuple(a + b for a, b in zip(coords_of(index), mirrored(cluster, shift))))


def layout():
    places, homes = [(0, 0, 0)], [(0, 0)]
    for number, (slots, shift) in enumerate(SENDS):
        for place, slot in enumerate(slots):
            places.append(tuple(a + b for a, b in zip(places[slot], shift)))
            homes.append((number + 1, place))
    return places, homes


def shift_pairs(shift, back, clusters, members):
    out = []
    for cluster in range(clusters):
        for index in range(members):
            other = cluster * members + moved(index, cluster, shift)
            here = cluster * members + index
            out.append((here, other) if back else (other, here))
    return out


def normalize_kernel(x_ref, out_ref):
    values = x_ref[...].astype(jnp.float32)
    scale = lax.rsqrt(jnp.sum(values * values, axis=1, keepdims=True) + 1e-06)
    out_ref[...] = (values * scale).astype(jnp.bfloat16)


def normalize(embeddings):
    return pl.pallas_call(
        normalize_kernel,
        out_shape=jax.ShapeDtypeStruct(embeddings.shape, jnp.bfloat16),
        in_specs=[pl.BlockSpec(memory_space=pltpu.VMEM)],
        out_specs=pl.BlockSpec(memory_space=pltpu.VMEM),
        compiler_params=pltpu.CompilerParams(vmem_limit_bytes=32 << 20),
        cost_estimate=pl.CostEstimate(flops=4 * embeddings.size, bytes_accessed=4 * embeddings.size, transcendentals=0),
    )(embeddings)


def gather_kernel(found_ref, out_ref):
    out_ref[...] = jnp.max(found_ref[...], axis=0)


def products(a, b):
    return lax.dot_general(a, b, (((1,), (1,)), ((), ())), preferred_element_type=jnp.float32)


def fold(scores):
    rows, columns = scores.shape
    return jnp.max(scores.reshape(rows // 8, 8, columns), axis=0)


def own_kernel(unit_ref, column_ref, row_ref, best_ref):
    best_ref[...] = jnp.full_like(best_ref, -1.0)
    earlier = column_ref[...] < row_ref[...]
    scores = products(unit_ref[...], unit_ref[...])
    best_ref[0] = fold(jnp.where(earlier, scores, jnp.float32(-1.0)))


def stage_kernel(slots, pairs, last, *refs):
    count = len(slots)
    order_ref, blocks, before_ref = refs[0], refs[1 : 1 + count], refs[1 + count]
    out, best = refs[2 + count :]
    best[...] = before_ref[...]
    for a, b in pairs:
        higher = order_ref[a] > order_ref[b]
        scores = products(blocks[slots.index(a)][...], blocks[slots.index(b)][...])
        best[b] = jnp.where(higher, best[b], jnp.maximum(best[b], fold(scores)))
        best[a] = jnp.where(higher, jnp.maximum(best[a], jnp.max(scores, axis=1)[None, :]), best[a])
    if last:
        out[...] = jnp.full_like(out, -1.0)
        for slot in range(best.shape[0]):
            out[order_ref[slot]] = jnp.max(best[slot], axis=0, keepdims=True)
    else:
        out[...] = best[...]


def call_kernel(kernel, shape, specs, scratch, products_done, *args):
    rows, width = 256, 768
    return pl.pallas_call(
        kernel,
        out_shape=jax.ShapeDtypeStruct(shape, jnp.float32),
        in_specs=specs,
        out_specs=pl.BlockSpec(memory_space=pltpu.VMEM),
        scratch_shapes=scratch,
        compiler_params=pltpu.CompilerParams(vmem_limit_bytes=32 << 20),
        cost_estimate=pl.CostEstimate(
            flops=2 * rows * rows * width * products_done,
            bytes_accessed=2 * rows * width * products_done,
            transcendentals=0,
        ),
    )(*args)


def per_device(clusters, members, embeddings, ranks):
    cluster, index = lax.axis_index("clusters"), lax.axis_index("members")
    places, _ = layout()
    order = jnp.stack([moved(index, cluster, place) for place in places])
    rows = embeddings.shape[0]
    total = len(places)
    smem = pl.BlockSpec(memory_space=pltpu.SMEM)
    vmem = pl.BlockSpec(memory_space=pltpu.VMEM)
    blocks = [normalize(embeddings)]
    best = call_kernel(
        own_kernel, (total, 8, rows), [vmem] * 3, [], 1, blocks[0], ranks.reshape(rows, 1), ranks.reshape(1, rows)
    )

    def compare(stage, best):
        pairs, last = STAGES[stage], stage == len(STAGES) - 1
        slots = sorted({s for pair in pairs for s in pair})

        def kernel(*refs):
            stage_kernel(slots, pairs, last, *refs)

        return call_kernel(
            kernel,
            (members, 1, rows) if last else (total, 8, rows),
            [smem] + [vmem] * (len(slots) + 1),
            [pltpu.VMEM((total, 8, rows), jnp.float32)],
            len(pairs),
            order,
            *[blocks[s] for s in slots],
            best,
        )

    for (slot,), shift in SENDS:
        if slot and len(blocks) == FIRST:
            blocks[HELD[0]], best, order = lax.optimization_barrier((blocks[HELD[0]], best, order))
            best = compare(0, best)
            blocks[HELD[1]], best = lax.optimization_barrier((blocks[HELD[1]], best))
        blocks.append(lax.ppermute(blocks[slot], BOTH, shift_pairs(shift, False, clusters, members)))
    for stage in range(1, len(STAGES)):
        best = compare(stage, best)
    found = lax.all_to_all(best, "members", 0, 0, tiled=True)
    return call_kernel(gather_kernel, (1, rows), [vmem], [], 0, found)[0]


def solution(mesh):
    clusters, members = mesh.shape["clusters"], mesh.shape["members"]
    in_specs = (P(BOTH, None), P(BOTH))

    def body(embeddings, ranks):
        return per_device(clusters, members, embeddings, ranks)

    return jax.shard_map(body, mesh=mesh, in_specs=in_specs, out_specs=P(BOTH), check_vma=False)
```

```python
import jax
import jax.numpy as jnp
from jax import lax
from jax.experimental import pallas as pl
from jax.experimental.pallas import tpu as pltpu
from jax.sharding import PartitionSpec as P

SIZES = (2, 8, 4)
SENDS = [((0,), (0, 2, 0)), ((0,), (1, 0, 1)), ((0,), (0, 0, -1)), ((0,), (0, 0, 1)), ((0,), (0, 1, 0)), ((1,), (0, 1, 0)), ((4,), (0, 0, 1)), ((3,), (1, 0, 0)), ((2,), (0, 0, 1)), ((2,), (0, 0, -1)), ((6,), (0, 1, 0))]
ROWS = [5, 1, 6]
STAGES = [[(1, 0), (2, 0), (2, 1)], [(3, 0), (3, 1), (3, 2), (4, 1), (4, 2), (4, 3), (5, 0), (5, 2), (5, 3), (5, 4)], [(6, 0), (6, 2), (6, 3), (6, 4), (7, 1), (7, 5), (7, 6), (8, 1), (8, 5), (8, 6)], [(11, 0), (11, 2), (11, 3), (11, 4), (11, 7), (11, 8), (11, 9), (11, 10), (9, 1), (9, 5), (9, 6), (10, 1), (10, 5), (10, 6)]]
FIRST = 6
HELD = (1, 6)
BOTH = ("clusters", "members")


def member(coords):
    x, z, y = coords
    return ((x % SIZES[0]) * SIZES[1] + z % SIZES[1]) * SIZES[2] + y % SIZES[2]


def coords_of(index):
    return index // (SIZES[1] * SIZES[2]), (index // SIZES[2]) % SIZES[1], index % SIZES[2]


def mirrored(cluster, shift):
    sign = 1 - 2 * (cluster % 2)
    return shift[0], sign * shift[1], sign * shift[2]


def moved(index, cluster, shift):
    return member(tuple(a + b for a, b in zip(coords_of(index), mirrored(cluster, shift))))


def layout():
    places, homes = [(0, 0, 0)], [(0, 0)]
    for number, (slots, shift) in enumerate(SENDS):
        for place, slot in enumerate(slots):
            places.append(tuple(a + b for a, b in zip(places[slot], shift)))
            homes.append((number + 1, place))
    return places, homes


def shift_pairs(shift, back, clusters, members):
    out = []
    for cluster in range(clusters):
        for index in range(members):
            other = cluster * members + moved(index, cluster, shift)
            here = cluster * members + index
            out.append((here, other) if back else (other, here))
    return out


def normalize_kernel(x_ref, out_ref):
    values = x_ref[...].astype(jnp.float32)
    scale = lax.rsqrt(jnp.sum(values * values, axis=1, keepdims=True) + 1e-06)
    out_ref[...] = (values * scale).astype(jnp.bfloat16)


def normalize(embeddings):
    return pl.pallas_call(
        normalize_kernel,
        out_shape=jax.ShapeDtypeStruct(embeddings.shape, jnp.bfloat16),
        in_specs=[pl.BlockSpec(memory_space=pltpu.VMEM)],
        out_specs=pl.BlockSpec(memory_space=pltpu.VMEM),
        compiler_params=pltpu.CompilerParams(vmem_limit_bytes=32 << 20),
        cost_estimate=pl.CostEstimate(flops=4 * embeddings.size, bytes_accessed=4 * embeddings.size, transcendentals=0),
    )(embeddings)


def gather_kernel(found_ref, *refs):
    best = jnp.max(found_ref[...], axis=0)
    for ref in refs[:-1]:
        best = jnp.maximum(best, ref[...])
    refs[-1][...] = best


def plane_groups(members):
    groups = [[m for m in range(members) if coords_of(m)[1] == z] for z in range(SIZES[1])]
    return groups


def place_in_group(member_index):
    plane = SIZES[1] * SIZES[2]
    return lax.div(member_index, plane) * SIZES[2] + lax.rem(member_index, SIZES[2])


def products(a, b):
    return lax.dot_general(a, b, (((1,), (1,)), ((), ())), preferred_element_type=jnp.float32)


def fold(scores):
    rows, columns = scores.shape
    return jnp.max(scores.reshape(rows // 8, 8, columns), axis=0)


def own_kernel(unit_ref, column_ref, row_ref, best_ref):
    best_ref[...] = jnp.full_like(best_ref, -1.0)
    earlier = column_ref[...] < row_ref[...]
    scores = products(unit_ref[...], unit_ref[...])
    best_ref[0] = fold(jnp.where(earlier, scores, jnp.float32(-1.0)))


def stage_kernel(slots, pairs, last, *refs):
    count = len(slots)
    order_ref, blocks, before_ref = refs[0], refs[1 : 1 + count], refs[1 + count]
    *outs, best = refs[2 + count :]
    out = outs[0]
    best[...] = before_ref[...]
    for a, b in pairs:
        higher = order_ref[a] > order_ref[b]
        scores = products(blocks[slots.index(a)][...], blocks[slots.index(b)][...])
        best[b] = jnp.where(higher, best[b], jnp.maximum(best[b], fold(scores)))
        best[a] = jnp.where(higher, jnp.maximum(best[a], jnp.max(scores, axis=1)[None, :]), best[a])
    if last:
        out[...] = jnp.full_like(out, -1.0)
        places = layout()[0]
        for slot in range(best.shape[0]):
            row = jnp.max(best[slot], axis=0, keepdims=True)
            if places[slot][1] == 0:
                out[place_in_group(order_ref[slot])] = row
            elif slot in ROWS:
                outs[1 + ROWS.index(slot)][...] = row
    else:
        out[...] = best[...]


def call_kernel(kernel, shapes, specs, scratch, products_done, *args):
    rows, width = 256, 768
    return pl.pallas_call(
        kernel,
        out_shape=[jax.ShapeDtypeStruct(one, jnp.float32) for one in shapes],
        in_specs=specs,
        out_specs=[pl.BlockSpec(memory_space=pltpu.VMEM)] * len(shapes),
        scratch_shapes=scratch,
        compiler_params=pltpu.CompilerParams(vmem_limit_bytes=32 << 20),
        cost_estimate=pl.CostEstimate(
            flops=2 * rows * rows * width * products_done,
            bytes_accessed=2 * rows * width * products_done,
            transcendentals=0,
        ),
    )(*args)


def per_device(clusters, members, embeddings, ranks):
    cluster, index = lax.axis_index("clusters"), lax.axis_index("members")
    places, _ = layout()
    order = jnp.stack([moved(index, cluster, place) for place in places])
    rows = embeddings.shape[0]
    total = len(places)
    plane = members // SIZES[1]
    smem = pl.BlockSpec(memory_space=pltpu.SMEM)
    vmem = pl.BlockSpec(memory_space=pltpu.VMEM)
    blocks = [normalize(embeddings)]
    (best,) = call_kernel(
        own_kernel, [(total, 8, rows)], [vmem] * 3, [], 1, blocks[0], ranks.reshape(rows, 1), ranks.reshape(1, rows)
    )

    def compare(stage, best):
        pairs, last = STAGES[stage], stage == len(STAGES) - 1
        slots = sorted({s for pair in pairs for s in pair})

        def kernel(*refs):
            stage_kernel(slots, pairs, last, *refs)

        return call_kernel(
            kernel,
            [(plane, 1, rows)] + [(1, rows)] * len(ROWS) if last else [(total, 8, rows)],
            [smem] + [vmem] * (len(slots) + 1),
            [pltpu.VMEM((total, 8, rows), jnp.float32)],
            len(pairs),
            order,
            *[blocks[s] for s in slots],
            best,
        )

    held = list(HELD)
    for (slot,), shift in SENDS:
        if slot and len(blocks) == FIRST:
            early = held.pop(0)
            blocks[early], best, order = lax.optimization_barrier((blocks[early], best, order))
        if slot in held:
            held.remove(slot)
            (best,) = compare(0, best)
            blocks[slot], best = lax.optimization_barrier((blocks[slot], best))
        blocks.append(lax.ppermute(blocks[slot], BOTH, shift_pairs(shift, False, clusters, members)))
    for stage in range(1, len(STAGES)):
        best, *rest = compare(stage, best)
    backs = [
        lax.ppermute(row, BOTH, shift_pairs(places[slot], True, clusters, members))
        for row, slot in zip(rest, ROWS)
    ]
    found = lax.all_to_all(best, "members", 0, 0, axis_index_groups=plane_groups(members), tiled=True)
    (result,) = call_kernel(gather_kernel, [(1, rows)], [vmem] * (1 + len(ROWS)), [], 0, found, *backs)
    return result[0]


def solution(mesh):
    clusters, members = mesh.shape["clusters"], mesh.shape["members"]
    in_specs = (P(BOTH, None), P(BOTH))

    def body(embeddings, ranks):
        return per_device(clusters, members, embeddings, ranks)

    return jax.shard_map(body, mesh=mesh, in_specs=in_specs, out_specs=P(BOTH), check_vma=False)
```

```python
import jax
import jax.numpy as jnp
from jax import lax
from jax.experimental import pallas as pl
from jax.experimental.pallas import tpu as pltpu
from jax.sharding import PartitionSpec as P

SIZES = (2, 8, 4)
SENDS = [((0,), (0, 2, 0)), ((0,), (1, 0, 1)), ((0,), (0, 0, -1)), ((0,), (0, 0, 1)), ((0,), (0, 1, 0)), ((1,), (0, 1, 0)), ((4,), (0, 0, 1)), ((3,), (1, 0, 0)), ((2,), (0, 0, 1)), ((2,), (0, 0, -1)), ((6,), (0, 1, 0))]
ROWS = [5, 1, 6]
STAGES = [[(1, 0), (5, 0)], [(2, 0), (2, 1), (3, 0), (3, 1), (3, 2), (4, 1), (4, 2), (4, 3), (5, 2), (5, 3), (5, 4)], [(6, 0), (6, 2), (6, 3), (6, 4), (7, 1), (7, 5), (7, 6), (8, 1), (8, 5), (8, 6)], [(9, 1), (9, 5), (9, 6), (10, 1), (10, 5), (10, 6)], [(11, 0), (11, 2), (11, 3), (11, 4), (11, 7), (11, 8), (11, 9), (11, 10)]]
FIRST = 6
HELD = (1, 6)
BOTH = ("clusters", "members")


def member(coords):
    x, z, y = coords
    return ((x % SIZES[0]) * SIZES[1] + z % SIZES[1]) * SIZES[2] + y % SIZES[2]


def coords_of(index):
    return index // (SIZES[1] * SIZES[2]), (index // SIZES[2]) % SIZES[1], index % SIZES[2]


def mirrored(cluster, shift):
    sign = 1 - 2 * (cluster % 2)
    return shift[0], sign * shift[1], sign * shift[2]


def moved(index, cluster, shift):
    return member(tuple(a + b for a, b in zip(coords_of(index), mirrored(cluster, shift))))


def layout():
    places, homes = [(0, 0, 0)], [(0, 0)]
    for number, (slots, shift) in enumerate(SENDS):
        for place, slot in enumerate(slots):
            places.append(tuple(a + b for a, b in zip(places[slot], shift)))
            homes.append((number + 1, place))
    return places, homes


def shift_pairs(shift, back, clusters, members):
    out = []
    for cluster in range(clusters):
        for index in range(members):
            other = cluster * members + moved(index, cluster, shift)
            here = cluster * members + index
            out.append((here, other) if back else (other, here))
    return out


def normalize_kernel(x_ref, out_ref):
    values = x_ref[...].astype(jnp.float32)
    scale = lax.rsqrt(jnp.sum(values * values, axis=1, keepdims=True) + 1e-06)
    out_ref[...] = (values * scale).astype(jnp.bfloat16)


def normalize(embeddings):
    return pl.pallas_call(
        normalize_kernel,
        out_shape=jax.ShapeDtypeStruct(embeddings.shape, jnp.bfloat16),
        in_specs=[pl.BlockSpec(memory_space=pltpu.VMEM)],
        out_specs=pl.BlockSpec(memory_space=pltpu.VMEM),
        compiler_params=pltpu.CompilerParams(vmem_limit_bytes=32 << 20),
        cost_estimate=pl.CostEstimate(flops=4 * embeddings.size, bytes_accessed=4 * embeddings.size, transcendentals=0),
    )(embeddings)


def gather_kernel(found_ref, *refs):
    best = jnp.max(found_ref[...], axis=0)
    for ref in refs[:-1]:
        best = jnp.maximum(best, ref[...])
    refs[-1][...] = best


def plane_groups(members):
    groups = [[m for m in range(members) if coords_of(m)[1] == z] for z in range(SIZES[1])]
    return groups


def place_in_group(member_index):
    plane = SIZES[1] * SIZES[2]
    return lax.div(member_index, plane) * SIZES[2] + lax.rem(member_index, SIZES[2])


def products(a, b):
    return lax.dot_general(a, b, (((1,), (1,)), ((), ())), preferred_element_type=jnp.float32)


def fold(scores):
    rows, columns = scores.shape
    return jnp.max(scores.reshape(rows // 8, 8, columns), axis=0)


def own_kernel(unit_ref, column_ref, row_ref, best_ref):
    best_ref[...] = jnp.full_like(best_ref, -1.0)
    earlier = column_ref[...] < row_ref[...]
    scores = products(unit_ref[...], unit_ref[...])
    best_ref[0] = fold(jnp.where(earlier, scores, jnp.float32(-1.0)))


def stage_kernel(slots, pairs, last, *refs):
    count = len(slots)
    order_ref, blocks, before_ref = refs[0], refs[1 : 1 + count], refs[1 + count]
    *outs, best = refs[2 + count :]
    out = outs[0]
    best[...] = before_ref[...]
    for a, b in pairs:
        higher = order_ref[a] > order_ref[b]
        scores = products(blocks[slots.index(a)][...], blocks[slots.index(b)][...])
        best[b] = jnp.where(higher, best[b], jnp.maximum(best[b], fold(scores)))
        best[a] = jnp.where(higher, jnp.maximum(best[a], jnp.max(scores, axis=1)[None, :]), best[a])
    if last:
        out[...] = jnp.full_like(out, -1.0)
        places = layout()[0]
        for slot in range(best.shape[0]):
            row = jnp.max(best[slot], axis=0, keepdims=True)
            if places[slot][1] == 0:
                out[place_in_group(order_ref[slot])] = row
            elif slot in ROWS:
                outs[1 + ROWS.index(slot)][...] = row
    else:
        out[...] = best[...]


def call_kernel(kernel, shapes, specs, scratch, products_done, *args):
    rows, width = 256, 768
    return pl.pallas_call(
        kernel,
        out_shape=[jax.ShapeDtypeStruct(one, jnp.float32) for one in shapes],
        in_specs=specs,
        out_specs=[pl.BlockSpec(memory_space=pltpu.VMEM)] * len(shapes),
        scratch_shapes=scratch,
        compiler_params=pltpu.CompilerParams(vmem_limit_bytes=32 << 20),
        cost_estimate=pl.CostEstimate(
            flops=2 * rows * rows * width * products_done,
            bytes_accessed=2 * rows * width * products_done,
            transcendentals=0,
        ),
    )(*args)


def per_device(clusters, members, embeddings, ranks):
    cluster, index = lax.axis_index("clusters"), lax.axis_index("members")
    places, _ = layout()
    order = jnp.stack([moved(index, cluster, place) for place in places])
    rows = embeddings.shape[0]
    total = len(places)
    plane = members // SIZES[1]
    smem = pl.BlockSpec(memory_space=pltpu.SMEM)
    vmem = pl.BlockSpec(memory_space=pltpu.VMEM)
    blocks = [normalize(embeddings)]
    (best,) = call_kernel(
        own_kernel, [(total, 8, rows)], [vmem] * 3, [], 1, blocks[0], ranks.reshape(rows, 1), ranks.reshape(1, rows)
    )

    def compare(stage, best):
        pairs, last = STAGES[stage], stage == len(STAGES) - 1
        slots = sorted({s for pair in pairs for s in pair})

        def kernel(*refs):
            stage_kernel(slots, pairs, last, *refs)

        return call_kernel(
            kernel,
            [(plane, 1, rows)] + [(1, rows)] * len(ROWS) if last else [(total, 8, rows)],
            [smem] + [vmem] * (len(slots) + 1),
            [pltpu.VMEM((total, 8, rows), jnp.float32)],
            len(pairs),
            order,
            *[blocks[s] for s in slots],
            best,
        )

    held = list(HELD)
    for (slot,), shift in SENDS:
        if slot and len(blocks) == FIRST:
            early = held.pop(0)
            blocks[early], best, order = lax.optimization_barrier((blocks[early], best, order))
        if slot in held:
            held.remove(slot)
            (best,) = compare(0, best)
            blocks[slot], best = lax.optimization_barrier((blocks[slot], best))
        blocks.append(lax.ppermute(blocks[slot], BOTH, shift_pairs(shift, False, clusters, members)))
    for stage in range(1, len(STAGES)):
        best, *rest = compare(stage, best)
    backs = [
        lax.ppermute(row, BOTH, shift_pairs(places[slot], True, clusters, members))
        for row, slot in zip(rest, ROWS)
    ]
    found = lax.all_to_all(best, "members", 0, 0, axis_index_groups=plane_groups(members), tiled=True)
    (result,) = call_kernel(gather_kernel, [(1, rows)], [vmem] * (1 + len(ROWS)), [], 0, found, *backs)
    return result[0]


def solution(mesh):
    clusters, members = mesh.shape["clusters"], mesh.shape["members"]
    in_specs = (P(BOTH, None), P(BOTH))

    def body(embeddings, ranks):
        return per_device(clusters, members, embeddings, ranks)

    return jax.shard_map(body, mesh=mesh, in_specs=in_specs, out_specs=P(BOTH), check_vma=False)
```

```python
import jax
import jax.numpy as jnp
from jax import lax
from jax.experimental import pallas as pl
from jax.experimental.pallas import tpu as pltpu
from jax.sharding import PartitionSpec as P

SIZES = (2, 8, 4)
SENDS = [((0,), (0, 2, 0)), ((0,), (1, 0, 1)), ((0,), (0, 0, -1)), ((0,), (0, 0, 1)), ((0,), (0, 1, 0)), ((1,), (0, 1, 0)), ((4,), (0, 0, 1)), ((3,), (1, 0, 0)), ((2,), (0, 0, 1)), ((2,), (0, 0, -1)), ((6,), (0, 1, 0))]
ROWS = [5, 1, 6]
STAGES = [[(1, 0), (2, 0), (2, 1), (3, 0), (3, 1), (3, 2), (4, 1), (4, 2), (4, 3), (5, 0), (5, 2), (5, 3), (5, 4)], [(6, 0), (6, 2), (6, 3), (6, 4), (7, 1), (7, 5), (7, 6), (8, 1), (8, 5), (8, 6)], [(9, 1), (9, 5), (9, 6), (10, 1), (10, 5), (10, 6)], [(11, 0), (11, 2), (11, 3), (11, 4), (11, 7), (11, 8), (11, 9), (11, 10)]]
FIRST = 6
HELD = (1,)
BOTH = ("clusters", "members")


def member(coords):
    x, z, y = coords
    return ((x % SIZES[0]) * SIZES[1] + z % SIZES[1]) * SIZES[2] + y % SIZES[2]


def coords_of(index):
    return index // (SIZES[1] * SIZES[2]), (index // SIZES[2]) % SIZES[1], index % SIZES[2]


def mirrored(cluster, shift):
    sign = 1 - 2 * (cluster % 2)
    return shift[0], sign * shift[1], sign * shift[2]


def moved(index, cluster, shift):
    return member(tuple(a + b for a, b in zip(coords_of(index), mirrored(cluster, shift))))


def layout():
    places, homes = [(0, 0, 0)], [(0, 0)]
    for number, (slots, shift) in enumerate(SENDS):
        for place, slot in enumerate(slots):
            places.append(tuple(a + b for a, b in zip(places[slot], shift)))
            homes.append((number + 1, place))
    return places, homes


def shift_pairs(shift, back, clusters, members):
    out = []
    for cluster in range(clusters):
        for index in range(members):
            other = cluster * members + moved(index, cluster, shift)
            here = cluster * members + index
            out.append((here, other) if back else (other, here))
    return out


def normalize_kernel(x_ref, out_ref):
    values = x_ref[...].astype(jnp.float32)
    scale = lax.rsqrt(jnp.sum(values * values, axis=1, keepdims=True) + 1e-06)
    out_ref[...] = (values * scale).astype(jnp.bfloat16)


def normalize(embeddings):
    return pl.pallas_call(
        normalize_kernel,
        out_shape=jax.ShapeDtypeStruct(embeddings.shape, jnp.bfloat16),
        in_specs=[pl.BlockSpec(memory_space=pltpu.VMEM)],
        out_specs=pl.BlockSpec(memory_space=pltpu.VMEM),
        compiler_params=pltpu.CompilerParams(vmem_limit_bytes=32 << 20),
        cost_estimate=pl.CostEstimate(flops=4 * embeddings.size, bytes_accessed=4 * embeddings.size, transcendentals=0),
    )(embeddings)


def gather_kernel(found_ref, *refs):
    best = jnp.max(found_ref[...], axis=0)
    for ref in refs[:-1]:
        best = jnp.maximum(best, ref[...])
    refs[-1][...] = best


def plane_groups(members):
    groups = [[m for m in range(members) if coords_of(m)[1] == z] for z in range(SIZES[1])]
    return groups


def place_in_group(member_index):
    plane = SIZES[1] * SIZES[2]
    return lax.div(member_index, plane) * SIZES[2] + lax.rem(member_index, SIZES[2])


def products(a, b):
    return lax.dot_general(a, b, (((1,), (1,)), ((), ())), preferred_element_type=jnp.float32)


def fold(scores):
    rows, columns = scores.shape
    return jnp.max(scores.reshape(rows // 8, 8, columns), axis=0)


def own_kernel(unit_ref, column_ref, row_ref, best_ref):
    best_ref[...] = jnp.full_like(best_ref, -1.0)
    earlier = column_ref[...] < row_ref[...]
    scores = products(unit_ref[...], unit_ref[...])
    best_ref[0] = fold(jnp.where(earlier, scores, jnp.float32(-1.0)))


def stage_kernel(slots, pairs, last, *refs):
    count = len(slots)
    order_ref, blocks, before_ref = refs[0], refs[1 : 1 + count], refs[1 + count]
    *outs, best = refs[2 + count :]
    out = outs[0]
    best[...] = before_ref[...]
    for a, b in pairs:
        higher = order_ref[a] > order_ref[b]
        scores = products(blocks[slots.index(a)][...], blocks[slots.index(b)][...])
        best[b] = jnp.where(higher, best[b], jnp.maximum(best[b], fold(scores)))
        best[a] = jnp.where(higher, jnp.maximum(best[a], jnp.max(scores, axis=1)[None, :]), best[a])
    if last:
        out[...] = jnp.full_like(out, -1.0)
        places = layout()[0]
        for slot in range(best.shape[0]):
            row = jnp.max(best[slot], axis=0, keepdims=True)
            if places[slot][1] == 0:
                out[place_in_group(order_ref[slot])] = row
            elif slot in ROWS:
                outs[1 + ROWS.index(slot)][...] = row
    else:
        out[...] = best[...]


def call_kernel(kernel, shapes, specs, scratch, products_done, *args):
    rows, width = 256, 768
    return pl.pallas_call(
        kernel,
        out_shape=[jax.ShapeDtypeStruct(one, jnp.float32) for one in shapes],
        in_specs=specs,
        out_specs=[pl.BlockSpec(memory_space=pltpu.VMEM)] * len(shapes),
        scratch_shapes=scratch,
        compiler_params=pltpu.CompilerParams(vmem_limit_bytes=32 << 20),
        cost_estimate=pl.CostEstimate(
            flops=2 * rows * rows * width * products_done,
            bytes_accessed=2 * rows * width * products_done,
            transcendentals=0,
        ),
    )(*args)


def per_device(clusters, members, embeddings, ranks):
    cluster, index = lax.axis_index("clusters"), lax.axis_index("members")
    places, _ = layout()
    order = jnp.stack([moved(index, cluster, place) for place in places])
    rows = embeddings.shape[0]
    total = len(places)
    plane = members // SIZES[1]
    smem = pl.BlockSpec(memory_space=pltpu.SMEM)
    vmem = pl.BlockSpec(memory_space=pltpu.VMEM)
    blocks = [normalize(embeddings)]
    (best,) = call_kernel(
        own_kernel, [(total, 8, rows)], [vmem] * 3, [], 1, blocks[0], ranks.reshape(rows, 1), ranks.reshape(1, rows)
    )

    def compare(stage, best):
        pairs, last = STAGES[stage], stage == len(STAGES) - 1
        slots = sorted({s for pair in pairs for s in pair})

        def kernel(*refs):
            stage_kernel(slots, pairs, last, *refs)

        return call_kernel(
            kernel,
            [(plane, 1, rows)] + [(1, rows)] * len(ROWS) if last else [(total, 8, rows)],
            [smem] + [vmem] * (len(slots) + 1),
            [pltpu.VMEM((total, 8, rows), jnp.float32)],
            len(pairs),
            order,
            *[blocks[s] for s in slots],
            best,
        )

    held = list(HELD)
    for (slot,), shift in SENDS:
        if slot and len(blocks) == FIRST:
            early = held.pop(0)
            blocks[early], best, order = lax.optimization_barrier((blocks[early], best, order))
        if slot in held:
            held.remove(slot)
            (best,) = compare(0, best)
            blocks[slot], best = lax.optimization_barrier((blocks[slot], best))
        blocks.append(lax.ppermute(blocks[slot], BOTH, shift_pairs(shift, False, clusters, members)))
    for stage in range(len(HELD) - 1, len(STAGES)):
        best, *rest = compare(stage, best)
    backs = [
        lax.ppermute(row, BOTH, shift_pairs(places[slot], True, clusters, members))
        for row, slot in zip(rest, ROWS)
    ]
    found = lax.all_to_all(best, "members", 0, 0, axis_index_groups=plane_groups(members), tiled=True)
    (result,) = call_kernel(gather_kernel, [(1, rows)], [vmem] * (1 + len(ROWS)), [], 0, found, *backs)
    return result[0]


def solution(mesh):
    clusters, members = mesh.shape["clusters"], mesh.shape["members"]
    in_specs = (P(BOTH, None), P(BOTH))

    def body(embeddings, ranks):
        return per_device(clusters, members, embeddings, ranks)

    return jax.shard_map(body, mesh=mesh, in_specs=in_specs, out_specs=P(BOTH), check_vma=False)
```

```python
import jax
import jax.numpy as jnp
from jax import lax
from jax.experimental import pallas as pl
from jax.experimental.pallas import tpu as pltpu
from jax.sharding import PartitionSpec as P

SIZES = (2, 8, 4)
SENDS = [((0,), (0, 2, 0)), ((0,), (1, 0, 1)), ((0,), (0, 0, -1)), ((0,), (0, 0, 1)), ((0,), (0, 1, 0)), ((1,), (0, 1, 0)), ((4,), (0, 0, 1)), ((3,), (1, 0, 0)), ((2,), (0, 0, 1)), ((2,), (0, 0, -1)), ((6,), (0, 1, 0))]
ROWS = [5, 1, 6]
STAGES = [[(1, 0), (2, 0), (2, 1), (3, 0), (3, 1), (3, 2), (4, 1), (4, 2), (4, 3), (5, 0), (5, 2), (5, 3), (5, 4)], [(6, 0), (6, 2), (6, 3), (6, 4), (7, 1), (7, 5), (7, 6), (8, 1), (8, 5), (8, 6)], [(9, 1), (9, 5), (9, 6), (10, 1), (10, 5), (10, 6)], [(11, 0), (11, 2), (11, 3), (11, 4), (11, 7), (11, 8), (11, 9), (11, 10)]]
FIRST = 6
HELD = (1,)
BOTH = ("clusters", "members")


def member(coords):
    x, z, y = coords
    return ((x % SIZES[0]) * SIZES[1] + z % SIZES[1]) * SIZES[2] + y % SIZES[2]


def coords_of(index):
    return index // (SIZES[1] * SIZES[2]), (index // SIZES[2]) % SIZES[1], index % SIZES[2]


def mirrored(cluster, shift):
    sign = 1 - 2 * (cluster % 2)
    return shift[0], sign * shift[1], sign * shift[2]


def moved(index, cluster, shift):
    return member(tuple(a + b for a, b in zip(coords_of(index), mirrored(cluster, shift))))


def layout():
    places, homes = [(0, 0, 0)], [(0, 0)]
    for number, (slots, shift) in enumerate(SENDS):
        for place, slot in enumerate(slots):
            places.append(tuple(a + b for a, b in zip(places[slot], shift)))
            homes.append((number + 1, place))
    return places, homes


def shift_pairs(shift, back, clusters, members):
    out = []
    for cluster in range(clusters):
        for index in range(members):
            other = cluster * members + moved(index, cluster, shift)
            here = cluster * members + index
            out.append((here, other) if back else (other, here))
    return out


def normalize_kernel(x_ref, out_ref):
    values = x_ref[...].astype(jnp.float32)
    scale = lax.rsqrt(jnp.sum(values * values, axis=1, keepdims=True) + 1e-06)
    out_ref[...] = (values * scale).astype(jnp.bfloat16)


def normalize(embeddings):
    return pl.pallas_call(
        normalize_kernel,
        out_shape=jax.ShapeDtypeStruct(embeddings.shape, jnp.bfloat16),
        in_specs=[pl.BlockSpec(memory_space=pltpu.VMEM)],
        out_specs=pl.BlockSpec(memory_space=pltpu.VMEM),
        compiler_params=pltpu.CompilerParams(vmem_limit_bytes=32 << 20),
        cost_estimate=pl.CostEstimate(flops=4 * embeddings.size, bytes_accessed=4 * embeddings.size, transcendentals=0),
    )(embeddings)


def gather_kernel(found_ref, *refs):
    best = jnp.max(found_ref[...], axis=0)
    for ref in refs[:-1]:
        best = jnp.maximum(best, ref[...])
    refs[-1][...] = best


def plane_groups(members):
    groups = [[m for m in range(members) if coords_of(m)[1] == z] for z in range(SIZES[1])]
    return groups


def place_in_group(member_index):
    plane = SIZES[1] * SIZES[2]
    return lax.div(member_index, plane) * SIZES[2] + lax.rem(member_index, SIZES[2])


def products(a, b):
    return lax.dot_general(a, b, (((1,), (1,)), ((), ())), preferred_element_type=jnp.float32)


def fold(scores):
    rows, columns = scores.shape
    return jnp.max(scores.reshape(rows // 8, 8, columns), axis=0)


def own_kernel(unit_ref, column_ref, row_ref, best_ref):
    best_ref[...] = jnp.full_like(best_ref, -1.0)
    earlier = column_ref[...] < row_ref[...]
    scores = products(unit_ref[...], unit_ref[...])
    best_ref[0] = fold(jnp.where(earlier, scores, jnp.float32(-1.0)))


def stage_kernel(slots, pairs, last, *refs):
    count = len(slots)
    order_ref, blocks, before_ref = refs[0], refs[1 : 1 + count], refs[1 + count]
    *outs, best = refs[2 + count :]
    out = outs[0]
    best[...] = before_ref[...]
    for a, b in pairs:
        higher = order_ref[a] > order_ref[b]
        scores = products(blocks[slots.index(a)][...], blocks[slots.index(b)][...])
        best[b] = jnp.where(higher, best[b], jnp.maximum(best[b], fold(scores)))
        best[a] = jnp.where(higher, jnp.maximum(best[a], jnp.max(scores, axis=1)[None, :]), best[a])
    if last:
        out[...] = jnp.full_like(out, -1.0)
        places = layout()[0]
        for slot in range(best.shape[0]):
            row = jnp.max(best[slot], axis=0, keepdims=True)
            if places[slot][1] == 0:
                out[place_in_group(order_ref[slot])] = row
            elif slot in ROWS:
                outs[1 + ROWS.index(slot)][...] = row
    else:
        out[...] = best[...]


def call_kernel(kernel, shapes, specs, scratch, products_done, *args):
    rows, width = 256, 768
    return pl.pallas_call(
        kernel,
        out_shape=[jax.ShapeDtypeStruct(one, jnp.float32) for one in shapes],
        in_specs=specs,
        out_specs=[pl.BlockSpec(memory_space=pltpu.VMEM)] * len(shapes),
        scratch_shapes=scratch,
        compiler_params=pltpu.CompilerParams(vmem_limit_bytes=32 << 20),
        cost_estimate=pl.CostEstimate(
            flops=2 * rows * rows * width * products_done,
            bytes_accessed=2 * rows * width * products_done,
            transcendentals=0,
        ),
    )(*args)


def per_device(clusters, members, embeddings, ranks):
    cluster, index = lax.axis_index("clusters"), lax.axis_index("members")
    places, _ = layout()
    order = jnp.stack([moved(index, cluster, place) for place in places])
    rows = embeddings.shape[0]
    total = len(places)
    plane = members // SIZES[1]
    smem = pl.BlockSpec(memory_space=pltpu.SMEM)
    vmem = pl.BlockSpec(memory_space=pltpu.VMEM)
    blocks = [embeddings]
    units = {0: normalize(embeddings)}
    (best,) = call_kernel(
        own_kernel, [(total, 8, rows)], [vmem] * 3, [], 1, units[0], ranks.reshape(rows, 1), ranks.reshape(1, rows)
    )

    def compare(stage, best):
        pairs, last = STAGES[stage], stage == len(STAGES) - 1
        slots = sorted({s for pair in pairs for s in pair})
        new = [slot for slot in slots if slot not in units]
        *raw, best = lax.optimization_barrier((*[blocks[slot] for slot in new], best))
        units.update({slot: normalize(block) for slot, block in zip(new, raw)})

        def kernel(*refs):
            stage_kernel(slots, pairs, last, *refs)

        return call_kernel(
            kernel,
            [(plane, 1, rows)] + [(1, rows)] * len(ROWS) if last else [(total, 8, rows)],
            [smem] + [vmem] * (len(slots) + 1),
            [pltpu.VMEM((total, 8, rows), jnp.float32)],
            len(pairs),
            order,
            *[units[s] for s in slots],
            best,
        )

    held = list(HELD)
    for (slot,), shift in SENDS:
        if slot and len(blocks) == FIRST:
            early = held.pop(0)
            blocks[early], best, order = lax.optimization_barrier((blocks[early], best, order))
        if slot in held:
            held.remove(slot)
            (best,) = compare(0, best)
            blocks[slot], best = lax.optimization_barrier((blocks[slot], best))
        blocks.append(lax.ppermute(blocks[slot], BOTH, shift_pairs(shift, False, clusters, members)))
    for stage in range(len(HELD) - 1, len(STAGES)):
        best, *rest = compare(stage, best)
    backs = [
        lax.ppermute(row, BOTH, shift_pairs(places[slot], True, clusters, members))
        for row, slot in zip(rest, ROWS)
    ]
    found = lax.all_to_all(best, "members", 0, 0, axis_index_groups=plane_groups(members), tiled=True)
    (result,) = call_kernel(gather_kernel, [(1, rows)], [vmem] * (1 + len(ROWS)), [], 0, found, *backs)
    return result[0]


def solution(mesh):
    clusters, members = mesh.shape["clusters"], mesh.shape["members"]
    in_specs = (P(BOTH, None), P(BOTH))

    def body(embeddings, ranks):
        return per_device(clusters, members, embeddings, ranks)

    return jax.shard_map(body, mesh=mesh, in_specs=in_specs, out_specs=P(BOTH), check_vma=False)
```

```python
import jax
import jax.numpy as jnp
from jax import lax
from jax.experimental import pallas as pl
from jax.experimental.pallas import tpu as pltpu
from jax.sharding import PartitionSpec as P

SIZES = (2, 8, 4)
SENDS = [((0,), (0, 2, 0)), ((0,), (1, 0, 1)), ((0,), (0, 0, -1)), ((0,), (0, 0, 1)), ((0,), (0, 1, 0)), ((1,), (0, 1, 0)), ((4,), (0, 0, 1)), ((3,), (1, 0, 0)), ((2,), (0, 0, 1)), ((2,), (0, 0, -1)), ((6,), (0, 1, 0))]
ROWS = [5, 1, 6]
STAGES = [[(1, 0), (2, 0), (2, 1), (3, 0), (3, 1), (3, 2), (4, 1), (4, 2), (4, 3), (5, 0), (5, 2), (5, 3), (5, 4)], [(6, 0), (6, 2), (6, 3), (6, 4), (7, 1), (7, 5), (7, 6), (8, 1), (8, 5), (8, 6)], [(11, 0), (11, 2), (11, 3), (11, 4), (11, 7), (11, 8), (11, 9), (11, 10), (9, 1), (9, 5), (9, 6), (10, 1), (10, 5), (10, 6)]]
FIRST = 6
HELD = (1,)
BOTH = ("clusters", "members")


def member(coords):
    x, z, y = coords
    return ((x % SIZES[0]) * SIZES[1] + z % SIZES[1]) * SIZES[2] + y % SIZES[2]


def coords_of(index):
    return index // (SIZES[1] * SIZES[2]), (index // SIZES[2]) % SIZES[1], index % SIZES[2]


def mirrored(cluster, shift):
    sign = 1 - 2 * (cluster % 2)
    return shift[0], sign * shift[1], sign * shift[2]


def moved(index, cluster, shift):
    return member(tuple(a + b for a, b in zip(coords_of(index), mirrored(cluster, shift))))


def layout():
    places, homes = [(0, 0, 0)], [(0, 0)]
    for number, (slots, shift) in enumerate(SENDS):
        for place, slot in enumerate(slots):
            places.append(tuple(a + b for a, b in zip(places[slot], shift)))
            homes.append((number + 1, place))
    return places, homes


def shift_pairs(shift, back, clusters, members):
    out = []
    for cluster in range(clusters):
        for index in range(members):
            other = cluster * members + moved(index, cluster, shift)
            here = cluster * members + index
            out.append((here, other) if back else (other, here))
    return out


def normalize_kernel(x_ref, out_ref):
    values = x_ref[...].astype(jnp.float32)
    scale = lax.rsqrt(jnp.sum(values * values, axis=1, keepdims=True) + 1e-06)
    out_ref[...] = (values * scale).astype(jnp.bfloat16)


def normalize(embeddings):
    return pl.pallas_call(
        normalize_kernel,
        out_shape=jax.ShapeDtypeStruct(embeddings.shape, jnp.bfloat16),
        in_specs=[pl.BlockSpec(memory_space=pltpu.VMEM)],
        out_specs=pl.BlockSpec(memory_space=pltpu.VMEM),
        compiler_params=pltpu.CompilerParams(vmem_limit_bytes=32 << 20),
        cost_estimate=pl.CostEstimate(flops=4 * embeddings.size, bytes_accessed=4 * embeddings.size, transcendentals=0),
    )(embeddings)


def gather_kernel(found_ref, *refs):
    best = jnp.max(found_ref[...], axis=0)
    for ref in refs[:-1]:
        best = jnp.maximum(best, ref[...])
    refs[-1][...] = best


def plane_groups(members):
    groups = [[m for m in range(members) if coords_of(m)[1] == z] for z in range(SIZES[1])]
    return groups


def place_in_group(member_index):
    plane = SIZES[1] * SIZES[2]
    return lax.div(member_index, plane) * SIZES[2] + lax.rem(member_index, SIZES[2])


def products(a, b):
    return lax.dot_general(a, b, (((1,), (1,)), ((), ())), preferred_element_type=jnp.float32)


def fold(scores):
    rows, columns = scores.shape
    return jnp.max(scores.reshape(rows // 8, 8, columns), axis=0)


def own_kernel(unit_ref, column_ref, row_ref, best_ref):
    best_ref[...] = jnp.full_like(best_ref, -1.0)
    earlier = column_ref[...] < row_ref[...]
    scores = products(unit_ref[...], unit_ref[...])
    best_ref[0] = fold(jnp.where(earlier, scores, jnp.float32(-1.0)))


def stage_kernel(slots, pairs, last, *refs):
    count = len(slots)
    order_ref, blocks, before_ref = refs[0], refs[1 : 1 + count], refs[1 + count]
    *outs, best = refs[2 + count :]
    out = outs[0]
    best[...] = before_ref[...]
    for a, b in pairs:
        higher = order_ref[a] > order_ref[b]
        scores = products(blocks[slots.index(a)][...], blocks[slots.index(b)][...])
        best[b] = jnp.where(higher, best[b], jnp.maximum(best[b], fold(scores)))
        best[a] = jnp.where(higher, jnp.maximum(best[a], jnp.max(scores, axis=1)[None, :]), best[a])
    if last:
        out[...] = jnp.full_like(out, -1.0)
        places = layout()[0]
        for slot in range(best.shape[0]):
            row = jnp.max(best[slot], axis=0, keepdims=True)
            if places[slot][1] == 0:
                out[place_in_group(order_ref[slot])] = row
            elif slot in ROWS:
                outs[1 + ROWS.index(slot)][...] = row
    else:
        out[...] = best[...]


def call_kernel(kernel, shapes, specs, scratch, products_done, *args):
    rows, width = 256, 768
    return pl.pallas_call(
        kernel,
        out_shape=[jax.ShapeDtypeStruct(one, jnp.float32) for one in shapes],
        in_specs=specs,
        out_specs=[pl.BlockSpec(memory_space=pltpu.VMEM)] * len(shapes),
        scratch_shapes=scratch,
        compiler_params=pltpu.CompilerParams(vmem_limit_bytes=32 << 20),
        cost_estimate=pl.CostEstimate(
            flops=2 * rows * rows * width * products_done,
            bytes_accessed=2 * rows * width * products_done,
            transcendentals=0,
        ),
    )(*args)


def per_device(clusters, members, embeddings, ranks):
    cluster, index = lax.axis_index("clusters"), lax.axis_index("members")
    places, _ = layout()
    order = jnp.stack([moved(index, cluster, place) for place in places])
    rows = embeddings.shape[0]
    total = len(places)
    plane = members // SIZES[1]
    smem = pl.BlockSpec(memory_space=pltpu.SMEM)
    vmem = pl.BlockSpec(memory_space=pltpu.VMEM)
    blocks = [embeddings]
    units = {0: normalize(embeddings)}
    (best,) = call_kernel(
        own_kernel, [(total, 8, rows)], [vmem] * 3, [], 1, units[0], ranks.reshape(rows, 1), ranks.reshape(1, rows)
    )

    def compare(stage, best):
        pairs, last = STAGES[stage], stage == len(STAGES) - 1
        slots = sorted({s for pair in pairs for s in pair})
        new = [slot for slot in slots if slot not in units]
        *raw, best = lax.optimization_barrier((*[blocks[slot] for slot in new], best))
        units.update({slot: normalize(block) for slot, block in zip(new, raw)})

        def kernel(*refs):
            stage_kernel(slots, pairs, last, *refs)

        return call_kernel(
            kernel,
            [(plane, 1, rows)] + [(1, rows)] * len(ROWS) if last else [(total, 8, rows)],
            [smem] + [vmem] * (len(slots) + 1),
            [pltpu.VMEM((total, 8, rows), jnp.float32)],
            len(pairs),
            order,
            *[units[s] for s in slots],
            best,
        )

    held = list(HELD)
    for (slot,), shift in SENDS:
        if slot and len(blocks) == FIRST:
            early = held.pop(0)
            blocks[early], best, order = lax.optimization_barrier((blocks[early], best, order))
        if slot in held:
            held.remove(slot)
            (best,) = compare(0, best)
            blocks[slot], best = lax.optimization_barrier((blocks[slot], best))
        blocks.append(lax.ppermute(blocks[slot], BOTH, shift_pairs(shift, False, clusters, members)))
    for stage in range(len(HELD) - 1, len(STAGES)):
        best, *rest = compare(stage, best)
    backs = [
        lax.ppermute(row, BOTH, shift_pairs(places[slot], True, clusters, members))
        for row, slot in zip(rest, ROWS)
    ]
    found = lax.all_to_all(best, "members", 0, 0, axis_index_groups=plane_groups(members), tiled=True)
    (result,) = call_kernel(gather_kernel, [(1, rows)], [vmem] * (1 + len(ROWS)), [], 0, found, *backs)
    return result[0]


def solution(mesh):
    clusters, members = mesh.shape["clusters"], mesh.shape["members"]
    in_specs = (P(BOTH, None), P(BOTH))

    def body(embeddings, ranks):
        return per_device(clusters, members, embeddings, ranks)

    return jax.shard_map(body, mesh=mesh, in_specs=in_specs, out_specs=P(BOTH), check_vma=False)
```

```python
import jax
import jax.numpy as jnp
from jax import lax
from jax.experimental import pallas as pl
from jax.experimental.pallas import tpu as pltpu
from jax.sharding import PartitionSpec as P

SIZES = (2, 8, 4)
SENDS = [((0,), (0, 2, 0)), ((0,), (1, 0, 1)), ((0,), (0, 0, -1)), ((0,), (0, 0, 1)), ((0,), (0, 1, 0)), ((1,), (0, 1, 0)), ((4,), (0, 0, 1)), ((3,), (1, 0, 0)), ((2,), (0, 0, 1)), ((2,), (0, 0, -1)), ((6,), (0, 1, 0))]
ROWS = [6, 1, 5]
STAGES = [[(1, 0), (2, 0), (2, 1), (3, 0), (3, 1), (3, 2), (4, 1), (4, 2), (4, 3), (5, 0), (5, 2), (5, 3), (5, 4)], [(6, 0), (6, 2), (6, 3), (6, 4), (7, 1), (7, 5), (7, 6), (8, 1), (8, 5), (8, 6)], [(11, 0), (11, 2), (11, 3), (11, 4), (11, 7), (11, 8), (11, 9), (11, 10), (9, 1), (9, 5), (9, 6), (10, 1), (10, 5), (10, 6)]]
FIRST = 6
HELD = (1,)
BOTH = ("clusters", "members")


def member(coords):
    x, z, y = coords
    return ((x % SIZES[0]) * SIZES[1] + z % SIZES[1]) * SIZES[2] + y % SIZES[2]


def coords_of(index):
    return index // (SIZES[1] * SIZES[2]), (index // SIZES[2]) % SIZES[1], index % SIZES[2]


def mirrored(cluster, shift):
    sign = 1 - 2 * (cluster % 2)
    return shift[0], sign * shift[1], sign * shift[2]


def moved(index, cluster, shift):
    return member(tuple(a + b for a, b in zip(coords_of(index), mirrored(cluster, shift))))


def layout():
    places, homes = [(0, 0, 0)], [(0, 0)]
    for number, (slots, shift) in enumerate(SENDS):
        for place, slot in enumerate(slots):
            places.append(tuple(a + b for a, b in zip(places[slot], shift)))
            homes.append((number + 1, place))
    return places, homes


def shift_pairs(shift, back, clusters, members):
    out = []
    for cluster in range(clusters):
        for index in range(members):
            other = cluster * members + moved(index, cluster, shift)
            here = cluster * members + index
            out.append((here, other) if back else (other, here))
    return out


def normalize_kernel(x_ref, out_ref):
    values = x_ref[...].astype(jnp.float32)
    scale = lax.rsqrt(jnp.sum(values * values, axis=1, keepdims=True) + 1e-06)
    out_ref[...] = (values * scale).astype(jnp.bfloat16)


def normalize(embeddings):
    return pl.pallas_call(
        normalize_kernel,
        out_shape=jax.ShapeDtypeStruct(embeddings.shape, jnp.bfloat16),
        in_specs=[pl.BlockSpec(memory_space=pltpu.VMEM)],
        out_specs=pl.BlockSpec(memory_space=pltpu.VMEM),
        compiler_params=pltpu.CompilerParams(vmem_limit_bytes=32 << 20),
        cost_estimate=pl.CostEstimate(flops=4 * embeddings.size, bytes_accessed=4 * embeddings.size, transcendentals=0),
    )(embeddings)


def gather_kernel(found_ref, *refs):
    best = jnp.max(found_ref[...], axis=0)
    for ref in refs[:-1]:
        best = jnp.maximum(best, ref[...])
    refs[-1][...] = best


def plane_groups(members):
    groups = [[m for m in range(members) if coords_of(m)[1] == z] for z in range(SIZES[1])]
    return groups


def place_in_group(member_index):
    plane = SIZES[1] * SIZES[2]
    return lax.div(member_index, plane) * SIZES[2] + lax.rem(member_index, SIZES[2])


def products(a, b):
    return lax.dot_general(a, b, (((1,), (1,)), ((), ())), preferred_element_type=jnp.float32)


def fold(scores):
    rows, columns = scores.shape
    return jnp.max(scores.reshape(rows // 8, 8, columns), axis=0)


def own_kernel(unit_ref, column_ref, row_ref, best_ref):
    best_ref[...] = jnp.full_like(best_ref, -1.0)
    earlier = column_ref[...] < row_ref[...]
    scores = products(unit_ref[...], unit_ref[...])
    best_ref[0] = fold(jnp.where(earlier, scores, jnp.float32(-1.0)))


def stage_kernel(slots, pairs, last, *refs):
    count = len(slots)
    order_ref, blocks, before_ref = refs[0], refs[1 : 1 + count], refs[1 + count]
    *outs, best = refs[2 + count :]
    out = outs[0]
    best[...] = before_ref[...]
    for a, b in pairs:
        higher = order_ref[a] > order_ref[b]
        scores = products(blocks[slots.index(a)][...], blocks[slots.index(b)][...])
        best[b] = jnp.where(higher, best[b], jnp.maximum(best[b], fold(scores)))
        best[a] = jnp.where(higher, jnp.maximum(best[a], jnp.max(scores, axis=1)[None, :]), best[a])
    if last:
        out[...] = jnp.full_like(out, -1.0)
        places = layout()[0]
        for slot in range(best.shape[0]):
            row = jnp.max(best[slot], axis=0, keepdims=True)
            if places[slot][1] == 0:
                out[place_in_group(order_ref[slot])] = row
            elif slot in ROWS:
                outs[1 + ROWS.index(slot)][...] = row
    else:
        out[...] = best[...]


def call_kernel(kernel, shapes, specs, scratch, products_done, *args):
    rows, width = 256, 768
    return pl.pallas_call(
        kernel,
        out_shape=[jax.ShapeDtypeStruct(one, jnp.float32) for one in shapes],
        in_specs=specs,
        out_specs=[pl.BlockSpec(memory_space=pltpu.VMEM)] * len(shapes),
        scratch_shapes=scratch,
        compiler_params=pltpu.CompilerParams(vmem_limit_bytes=32 << 20),
        cost_estimate=pl.CostEstimate(
            flops=2 * rows * rows * width * products_done,
            bytes_accessed=2 * rows * width * products_done,
            transcendentals=0,
        ),
    )(*args)


def per_device(clusters, members, embeddings, ranks):
    cluster, index = lax.axis_index("clusters"), lax.axis_index("members")
    places, _ = layout()
    order = jnp.stack([moved(index, cluster, place) for place in places])
    rows = embeddings.shape[0]
    total = len(places)
    plane = members // SIZES[1]
    smem = pl.BlockSpec(memory_space=pltpu.SMEM)
    vmem = pl.BlockSpec(memory_space=pltpu.VMEM)
    blocks = [embeddings]
    units = {0: normalize(embeddings)}
    (best,) = call_kernel(
        own_kernel, [(total, 8, rows)], [vmem] * 3, [], 1, units[0], ranks.reshape(rows, 1), ranks.reshape(1, rows)
    )

    def compare(stage, best):
        pairs, last = STAGES[stage], stage == len(STAGES) - 1
        slots = sorted({s for pair in pairs for s in pair})
        new = [slot for slot in slots if slot not in units]
        *raw, best = lax.optimization_barrier((*[blocks[slot] for slot in new], best))
        units.update({slot: normalize(block) for slot, block in zip(new, raw)})

        def kernel(*refs):
            stage_kernel(slots, pairs, last, *refs)

        return call_kernel(
            kernel,
            [(plane, 1, rows)] + [(1, rows)] * len(ROWS) if last else [(total, 8, rows)],
            [smem] + [vmem] * (len(slots) + 1),
            [pltpu.VMEM((total, 8, rows), jnp.float32)],
            len(pairs),
            order,
            *[units[s] for s in slots],
            best,
        )

    held = list(HELD)
    for (slot,), shift in SENDS:
        if slot and len(blocks) == FIRST:
            early = held.pop(0)
            blocks[early], best, order = lax.optimization_barrier((blocks[early], best, order))
        if slot in held:
            held.remove(slot)
            (best,) = compare(0, best)
            blocks[slot], best = lax.optimization_barrier((blocks[slot], best))
        blocks.append(lax.ppermute(blocks[slot], BOTH, shift_pairs(shift, False, clusters, members)))
    for stage in range(len(HELD) - 1, len(STAGES)):
        best, *rest = compare(stage, best)
    backs = [
        lax.ppermute(row, BOTH, shift_pairs(places[slot], True, clusters, members))
        for row, slot in zip(rest, ROWS)
    ]
    found = lax.all_to_all(best, "members", 0, 0, axis_index_groups=plane_groups(members), tiled=True)
    (result,) = call_kernel(gather_kernel, [(1, rows)], [vmem] * (1 + len(ROWS)), [], 0, found, *backs)
    return result[0]


def solution(mesh):
    clusters, members = mesh.shape["clusters"], mesh.shape["members"]
    in_specs = (P(BOTH, None), P(BOTH))

    def body(embeddings, ranks):
        return per_device(clusters, members, embeddings, ranks)

    return jax.shard_map(body, mesh=mesh, in_specs=in_specs, out_specs=P(BOTH), check_vma=False)
```

```python
import jax
import jax.numpy as jnp
from jax import lax
from jax.experimental import pallas as pl
from jax.experimental.pallas import tpu as pltpu
from jax.sharding import PartitionSpec as P

SIZES = (2, 8, 4)
SENDS = [((0,), (0, 2, 0)), ((0,), (1, 0, 1)), ((0,), (0, 0, -1)), ((0,), (0, 0, 1)), ((0,), (0, 1, 0)), ((1,), (0, 1, 0)), ((4,), (0, 0, 1)), ((3,), (1, 0, 0)), ((2,), (0, 0, 1)), ((2,), (0, 0, -1)), ((6,), (0, 1, 0))]
ROWS = [6, 1, 5]
STAGES = [[(1, 0), (2, 0), (2, 1), (3, 0), (3, 1), (3, 2), (4, 1), (4, 2), (4, 3), (5, 0), (5, 2), (5, 3), (5, 4)], [(6, 0), (6, 2), (6, 3), (6, 4), (7, 1), (7, 5), (7, 6), (8, 1), (8, 5), (8, 6)], [(10, 1), (10, 5), (10, 6)], [(11, 0), (11, 2), (11, 3), (11, 4), (11, 7), (11, 8), (11, 9), (11, 10), (9, 1), (9, 5), (9, 6)]]
FIRST = 6
HELD = (1,)
BOTH = ("clusters", "members")


def member(coords):
    x, z, y = coords
    return ((x % SIZES[0]) * SIZES[1] + z % SIZES[1]) * SIZES[2] + y % SIZES[2]


def coords_of(index):
    return index // (SIZES[1] * SIZES[2]), (index // SIZES[2]) % SIZES[1], index % SIZES[2]


def mirrored(cluster, shift):
    sign = 1 - 2 * (cluster % 2)
    return shift[0], sign * shift[1], sign * shift[2]


def moved(index, cluster, shift):
    return member(tuple(a + b for a, b in zip(coords_of(index), mirrored(cluster, shift))))


def layout():
    places, homes = [(0, 0, 0)], [(0, 0)]
    for number, (slots, shift) in enumerate(SENDS):
        for place, slot in enumerate(slots):
            places.append(tuple(a + b for a, b in zip(places[slot], shift)))
            homes.append((number + 1, place))
    return places, homes


def shift_pairs(shift, back, clusters, members):
    out = []
    for cluster in range(clusters):
        for index in range(members):
            other = cluster * members + moved(index, cluster, shift)
            here = cluster * members + index
            out.append((here, other) if back else (other, here))
    return out


def normalize_kernel(x_ref, out_ref):
    values = x_ref[...].astype(jnp.float32)
    scale = lax.rsqrt(jnp.sum(values * values, axis=1, keepdims=True) + 1e-06)
    out_ref[...] = (values * scale).astype(jnp.bfloat16)


def normalize(embeddings):
    return pl.pallas_call(
        normalize_kernel,
        out_shape=jax.ShapeDtypeStruct(embeddings.shape, jnp.bfloat16),
        in_specs=[pl.BlockSpec(memory_space=pltpu.VMEM)],
        out_specs=pl.BlockSpec(memory_space=pltpu.VMEM),
        compiler_params=pltpu.CompilerParams(vmem_limit_bytes=32 << 20),
        cost_estimate=pl.CostEstimate(flops=4 * embeddings.size, bytes_accessed=4 * embeddings.size, transcendentals=0),
    )(embeddings)


def gather_kernel(found_ref, *refs):
    best = jnp.max(found_ref[...], axis=0)
    for ref in refs[:-1]:
        best = jnp.maximum(best, ref[...])
    refs[-1][...] = best


def plane_groups(members):
    groups = [[m for m in range(members) if coords_of(m)[1] == z] for z in range(SIZES[1])]
    return groups


def place_in_group(member_index):
    plane = SIZES[1] * SIZES[2]
    return lax.div(member_index, plane) * SIZES[2] + lax.rem(member_index, SIZES[2])


def products(a, b):
    return lax.dot_general(a, b, (((1,), (1,)), ((), ())), preferred_element_type=jnp.float32)


def fold(scores):
    rows, columns = scores.shape
    return jnp.max(scores.reshape(rows // 8, 8, columns), axis=0)


def own_kernel(unit_ref, column_ref, row_ref, best_ref):
    best_ref[...] = jnp.full_like(best_ref, -1.0)
    earlier = column_ref[...] < row_ref[...]
    scores = products(unit_ref[...], unit_ref[...])
    best_ref[0] = fold(jnp.where(earlier, scores, jnp.float32(-1.0)))


def stage_kernel(slots, pairs, last, *refs):
    count = len(slots)
    order_ref, blocks, before_ref = refs[0], refs[1 : 1 + count], refs[1 + count]
    *outs, best = refs[2 + count :]
    out = outs[0]
    best[...] = before_ref[...]
    for a, b in pairs:
        higher = order_ref[a] > order_ref[b]
        scores = products(blocks[slots.index(a)][...], blocks[slots.index(b)][...])
        best[b] = jnp.where(higher, best[b], jnp.maximum(best[b], fold(scores)))
        best[a] = jnp.where(higher, jnp.maximum(best[a], jnp.max(scores, axis=1)[None, :]), best[a])
    if last:
        out[...] = jnp.full_like(out, -1.0)
        places = layout()[0]
        for slot in range(best.shape[0]):
            row = jnp.max(best[slot], axis=0, keepdims=True)
            if places[slot][1] == 0:
                out[place_in_group(order_ref[slot])] = row
            elif slot in ROWS:
                outs[1 + ROWS.index(slot)][...] = row
    else:
        out[...] = best[...]


def call_kernel(kernel, shapes, specs, scratch, products_done, *args):
    rows, width = 256, 768
    return pl.pallas_call(
        kernel,
        out_shape=[jax.ShapeDtypeStruct(one, jnp.float32) for one in shapes],
        in_specs=specs,
        out_specs=[pl.BlockSpec(memory_space=pltpu.VMEM)] * len(shapes),
        scratch_shapes=scratch,
        compiler_params=pltpu.CompilerParams(vmem_limit_bytes=32 << 20),
        cost_estimate=pl.CostEstimate(
            flops=2 * rows * rows * width * products_done,
            bytes_accessed=2 * rows * width * products_done,
            transcendentals=0,
        ),
    )(*args)


def per_device(clusters, members, embeddings, ranks):
    cluster, index = lax.axis_index("clusters"), lax.axis_index("members")
    places, _ = layout()
    order = jnp.stack([moved(index, cluster, place) for place in places])
    rows = embeddings.shape[0]
    total = len(places)
    plane = members // SIZES[1]
    smem = pl.BlockSpec(memory_space=pltpu.SMEM)
    vmem = pl.BlockSpec(memory_space=pltpu.VMEM)
    blocks = [embeddings]
    units = {0: normalize(embeddings)}
    (best,) = call_kernel(
        own_kernel, [(total, 8, rows)], [vmem] * 3, [], 1, units[0], ranks.reshape(rows, 1), ranks.reshape(1, rows)
    )

    def compare(stage, best):
        pairs, last = STAGES[stage], stage == len(STAGES) - 1
        slots = sorted({s for pair in pairs for s in pair})
        new = [slot for slot in slots if slot not in units]
        *raw, best = lax.optimization_barrier((*[blocks[slot] for slot in new], best))
        units.update({slot: normalize(block) for slot, block in zip(new, raw)})

        def kernel(*refs):
            stage_kernel(slots, pairs, last, *refs)

        return call_kernel(
            kernel,
            [(plane, 1, rows)] + [(1, rows)] * len(ROWS) if last else [(total, 8, rows)],
            [smem] + [vmem] * (len(slots) + 1),
            [pltpu.VMEM((total, 8, rows), jnp.float32)],
            len(pairs),
            order,
            *[units[s] for s in slots],
            best,
        )

    held = list(HELD)
    for (slot,), shift in SENDS:
        if slot and len(blocks) == FIRST:
            early = held.pop(0)
            blocks[early], best, order = lax.optimization_barrier((blocks[early], best, order))
        if slot in held:
            held.remove(slot)
            (best,) = compare(0, best)
            blocks[slot], best = lax.optimization_barrier((blocks[slot], best))
        blocks.append(lax.ppermute(blocks[slot], BOTH, shift_pairs(shift, False, clusters, members)))
    for stage in range(len(HELD) - 1, len(STAGES)):
        best, *rest = compare(stage, best)
    backs = [
        lax.ppermute(row, BOTH, shift_pairs(places[slot], True, clusters, members))
        for row, slot in zip(rest, ROWS)
    ]
    found = lax.all_to_all(best, "members", 0, 0, axis_index_groups=plane_groups(members), tiled=True)
    (result,) = call_kernel(gather_kernel, [(1, rows)], [vmem] * (1 + len(ROWS)), [], 0, found, *backs)
    return result[0]


def solution(mesh):
    clusters, members = mesh.shape["clusters"], mesh.shape["members"]
    in_specs = (P(BOTH, None), P(BOTH))

    def body(embeddings, ranks):
        return per_device(clusters, members, embeddings, ranks)

    return jax.shard_map(body, mesh=mesh, in_specs=in_specs, out_specs=P(BOTH), check_vma=False)
```

```python
import jax
import jax.numpy as jnp
from jax import lax
from jax.experimental import pallas as pl
from jax.experimental.pallas import tpu as pltpu
from jax.sharding import PartitionSpec as P

SIZES = (2, 8, 4)
SENDS = [((0,), (0, 2, 0)), ((0,), (1, 0, 1)), ((0,), (0, 0, -1)), ((0,), (0, 0, 1)), ((0,), (0, 1, 0)), ((1,), (0, 1, 0)), ((4,), (0, 0, 1)), ((3,), (1, 0, 0)), ((2,), (0, 0, 1)), ((2,), (0, 0, -1)), ((6,), (0, 1, 0))]
ROWS = [6, 1, 5]
STAGES = [[(1, 0), (2, 0), (2, 1), (3, 0), (3, 1), (3, 2), (4, 1), (4, 2), (4, 3), (5, 0), (5, 2), (5, 3), (5, 4)], [(6, 0), (6, 2), (6, 3), (6, 4), (7, 1), (7, 5), (7, 6), (8, 1), (8, 5), (8, 6)], [(10, 1), (10, 5), (10, 6)], [(11, 0), (11, 2), (11, 3), (11, 4), (11, 7), (11, 8), (11, 10)], [(11, 9), (9, 1), (9, 5), (9, 6)]]
FIRST = 6
HELD = (1,)
BOTH = ("clusters", "members")


def member(coords):
    x, z, y = coords
    return ((x % SIZES[0]) * SIZES[1] + z % SIZES[1]) * SIZES[2] + y % SIZES[2]


def coords_of(index):
    return index // (SIZES[1] * SIZES[2]), (index // SIZES[2]) % SIZES[1], index % SIZES[2]


def mirrored(cluster, shift):
    sign = 1 - 2 * (cluster % 2)
    return shift[0], sign * shift[1], sign * shift[2]


def moved(index, cluster, shift):
    return member(tuple(a + b for a, b in zip(coords_of(index), mirrored(cluster, shift))))


def layout():
    places, homes = [(0, 0, 0)], [(0, 0)]
    for number, (slots, shift) in enumerate(SENDS):
        for place, slot in enumerate(slots):
            places.append(tuple(a + b for a, b in zip(places[slot], shift)))
            homes.append((number + 1, place))
    return places, homes


def shift_pairs(shift, back, clusters, members):
    out = []
    for cluster in range(clusters):
        for index in range(members):
            other = cluster * members + moved(index, cluster, shift)
            here = cluster * members + index
            out.append((here, other) if back else (other, here))
    return out


def normalize_kernel(x_ref, out_ref):
    values = x_ref[...].astype(jnp.float32)
    scale = lax.rsqrt(jnp.sum(values * values, axis=1, keepdims=True) + 1e-06)
    out_ref[...] = (values * scale).astype(jnp.bfloat16)


def normalize(embeddings):
    return pl.pallas_call(
        normalize_kernel,
        out_shape=jax.ShapeDtypeStruct(embeddings.shape, jnp.bfloat16),
        in_specs=[pl.BlockSpec(memory_space=pltpu.VMEM)],
        out_specs=pl.BlockSpec(memory_space=pltpu.VMEM),
        compiler_params=pltpu.CompilerParams(vmem_limit_bytes=32 << 20),
        cost_estimate=pl.CostEstimate(flops=4 * embeddings.size, bytes_accessed=4 * embeddings.size, transcendentals=0),
    )(embeddings)


def gather_kernel(found_ref, *refs):
    best = jnp.max(found_ref[...], axis=0)
    for ref in refs[:-1]:
        best = jnp.maximum(best, ref[...])
    refs[-1][...] = best


def plane_groups(members):
    groups = [[m for m in range(members) if coords_of(m)[1] == z] for z in range(SIZES[1])]
    return groups


def place_in_group(member_index):
    plane = SIZES[1] * SIZES[2]
    return lax.div(member_index, plane) * SIZES[2] + lax.rem(member_index, SIZES[2])


def products(a, b):
    return lax.dot_general(a, b, (((1,), (1,)), ((), ())), preferred_element_type=jnp.float32)


def fold(scores):
    rows, columns = scores.shape
    return jnp.max(scores.reshape(rows // 8, 8, columns), axis=0)


def own_kernel(unit_ref, column_ref, row_ref, best_ref):
    best_ref[...] = jnp.full_like(best_ref, -1.0)
    earlier = column_ref[...] < row_ref[...]
    scores = products(unit_ref[...], unit_ref[...])
    best_ref[0] = fold(jnp.where(earlier, scores, jnp.float32(-1.0)))


def stage_kernel(slots, pairs, last, *refs):
    count = len(slots)
    order_ref, blocks, before_ref = refs[0], refs[1 : 1 + count], refs[1 + count]
    *outs, best = refs[2 + count :]
    out = outs[0]
    best[...] = before_ref[...]
    for a, b in pairs:
        higher = order_ref[a] > order_ref[b]
        scores = products(blocks[slots.index(a)][...], blocks[slots.index(b)][...])
        best[b] = jnp.where(higher, best[b], jnp.maximum(best[b], fold(scores)))
        best[a] = jnp.where(higher, jnp.maximum(best[a], jnp.max(scores, axis=1)[None, :]), best[a])
    if last:
        out[...] = jnp.full_like(out, -1.0)
        places = layout()[0]
        for slot in range(best.shape[0]):
            row = jnp.max(best[slot], axis=0, keepdims=True)
            if places[slot][1] == 0:
                out[place_in_group(order_ref[slot])] = row
            elif slot in ROWS:
                outs[1 + ROWS.index(slot)][...] = row
    else:
        out[...] = best[...]


def call_kernel(kernel, shapes, specs, scratch, products_done, *args):
    rows, width = 256, 768
    return pl.pallas_call(
        kernel,
        out_shape=[jax.ShapeDtypeStruct(one, jnp.float32) for one in shapes],
        in_specs=specs,
        out_specs=[pl.BlockSpec(memory_space=pltpu.VMEM)] * len(shapes),
        scratch_shapes=scratch,
        compiler_params=pltpu.CompilerParams(vmem_limit_bytes=32 << 20),
        cost_estimate=pl.CostEstimate(
            flops=2 * rows * rows * width * products_done,
            bytes_accessed=2 * rows * width * products_done,
            transcendentals=0,
        ),
    )(*args)


def per_device(clusters, members, embeddings, ranks):
    cluster, index = lax.axis_index("clusters"), lax.axis_index("members")
    places, _ = layout()
    order = jnp.stack([moved(index, cluster, place) for place in places])
    rows = embeddings.shape[0]
    total = len(places)
    plane = members // SIZES[1]
    smem = pl.BlockSpec(memory_space=pltpu.SMEM)
    vmem = pl.BlockSpec(memory_space=pltpu.VMEM)
    blocks = [embeddings]
    units = {0: normalize(embeddings)}
    (best,) = call_kernel(
        own_kernel, [(total, 8, rows)], [vmem] * 3, [], 1, units[0], ranks.reshape(rows, 1), ranks.reshape(1, rows)
    )

    def compare(stage, best):
        pairs, last = STAGES[stage], stage == len(STAGES) - 1
        slots = sorted({s for pair in pairs for s in pair})
        new = [slot for slot in slots if slot not in units]
        *raw, best = lax.optimization_barrier((*[blocks[slot] for slot in new], best))
        units.update({slot: normalize(block) for slot, block in zip(new, raw)})

        def kernel(*refs):
            stage_kernel(slots, pairs, last, *refs)

        return call_kernel(
            kernel,
            [(plane, 1, rows)] + [(1, rows)] * len(ROWS) if last else [(total, 8, rows)],
            [smem] + [vmem] * (len(slots) + 1),
            [pltpu.VMEM((total, 8, rows), jnp.float32)],
            len(pairs),
            order,
            *[units[s] for s in slots],
            best,
        )

    held = list(HELD)
    for (slot,), shift in SENDS:
        if slot and len(blocks) == FIRST:
            early = held.pop(0)
            blocks[early], best, order = lax.optimization_barrier((blocks[early], best, order))
        if slot in held:
            held.remove(slot)
            (best,) = compare(0, best)
            blocks[slot], best = lax.optimization_barrier((blocks[slot], best))
        blocks.append(lax.ppermute(blocks[slot], BOTH, shift_pairs(shift, False, clusters, members)))
    for stage in range(len(HELD) - 1, len(STAGES)):
        best, *rest = compare(stage, best)
    backs = [
        lax.ppermute(row, BOTH, shift_pairs(places[slot], True, clusters, members))
        for row, slot in zip(rest, ROWS)
    ]
    found = lax.all_to_all(best, "members", 0, 0, axis_index_groups=plane_groups(members), tiled=True)
    (result,) = call_kernel(gather_kernel, [(1, rows)], [vmem] * (1 + len(ROWS)), [], 0, found, *backs)
    return result[0]


def solution(mesh):
    clusters, members = mesh.shape["clusters"], mesh.shape["members"]
    in_specs = (P(BOTH, None), P(BOTH))

    def body(embeddings, ranks):
        return per_device(clusters, members, embeddings, ranks)

    return jax.shard_map(body, mesh=mesh, in_specs=in_specs, out_specs=P(BOTH), check_vma=False)
```
